32 devices in a mesh: groups: 2 (over x), dp: 16 (over z, y, core).
Axes of the slice: x: 2, y: 2, z: 4, core: 2. Of those that a mesh axis runs over, the one named last changes fastest.
Arguments:
- res_lat: bfloat16 [256, 128, 512], P(('groups', 'dp')), parts along dimension 0, may hold values from -6 to 6
- res_rope: bfloat16 [256, 64, 128], P(('groups', 'dp')), parts along dimension 0, may hold values from -6 to 6
- res_table: int32 [32, 8], P(('groups', 'dp')), parts along dimension 0, may hold values from 0 to 7, each once within a row
- res_len: int32 [32], P(('groups', 'dp')), parts along dimension 0, may hold values from 1 to 1024
- out_lat: bfloat16 [256, 128, 512], P(('groups', 'dp')), parts along dimension 0, may hold values from -6 to 6
- out_rope: bfloat16 [256, 64, 128], P(('groups', 'dp')), parts along dimension 0, may hold values from -6 to 6
- out_fill: int32 [256], P(('groups', 'dp')), parts along dimension 0, may hold values from 1 to 128
- send_table: int32 [512], P(('groups', 'dp')), parts along dimension 0, may hold values from -1 to 7, as said below
- arr_index: int32 [480], P(('groups', 'dp')), parts along dimension 0, may hold values from 0 to 15, as said below
- arr_count: int32 [32], P(('groups', 'dp')), parts along dimension 0, may hold values from 1 to 15, as said below
- mig_lat: bfloat16 [384, 128, 512], P(('groups', 'dp')), parts along dimension 0, may hold values from -6 to 6
- mig_rope: bfloat16 [384, 64, 128], P(('groups', 'dp')), parts along dimension 0, may hold values from -6 to 6
- mig_len: int32 [32], P(('groups', 'dp')), parts along dimension 0, may hold values from 1 to 1536
- mig_bit: int32 [32], P(('groups', 'dp')), parts along dimension 0, may hold values from -1 to 3, as said below
- q_lat: bfloat16 [96, 4, 128, 512], P(('groups', 'dp')), parts along dimension 0, may hold values from -12 to 12
- q_rope: bfloat16 [96, 4, 64, 128], P(('groups', 'dp')), parts along dimension 0, may hold values from -6 to 6
- new_kv: bfloat16 [96, 4, 576], P(('groups', 'dp')), parts along dimension 0, may hold values from -6 to 6
Outputs:
- attended: bfloat16 [96, 4, 128, 512], P(('groups', 'dp')), parts along dimension 0
The draws below stay inside these ranges and needn't reach their ends.
There are 2 independent parts, one for each index of `groups`. The reference program is written for one: setup_inputs(seed, part) draws one part's arguments, and reference() takes and returns one part's arrays. A program takes and returns all parts, laid end to end along the dimension named above; each array names one. Nothing has to cross between parts.
Inputs may be any that keep to these rules, and one draw needn't show every extreme that they name: `mig_bit`: an entry b >= 0 pairs device i with device i XOR 2 ** b, whose entry is also b; -1 means the device has no partner. `send_table`: each source's 16 * 1 entries name each of its 8 blocks exactly once; the other entries are -1. `arr_index`: the first arr_count[o] entries of owner o name distinct slots s + c into which source s sends a block for o; later entries are 0. `arr_count`: the counts sum to 128.
All inputs are finite; a program needn't handle non-finite values.
Results may differ from the reference program's by a relative error of at most 0.0033.
Values may be sent and summed in bfloat16 or wider, within the bound.
A program may use at most 128 MiB of HBM per device.

```python
import jax
import jax.numpy as jnp
from jax import lax

H = 128
DL = 512
DR = 64
BLK = 128
STEPS = 4
RB = 8
MB = 12
REQ = 1
OUTB = 8
RESB = 8
CAP = 1
ARRB = 15
LOGDP = 4
N_DP = 16


def load_factor(key):
    return jax.random.randint(jax.random.fold_in(key, 5), (N_DP,), 1, 5)


def skewed_lengths(key, salt, per_device, longest):
    factor = load_factor(key)
    drawn = jax.random.randint(jax.random.fold_in(key, salt), (N_DP, per_device), 1, longest + 1)
    lengths = jnp.maximum(1, drawn * factor[:, None] // 4).reshape(-1)
    forced = jax.random.randint(jax.random.fold_in(key, salt + 1), (), 0, N_DP * per_device)
    return jnp.where(jnp.arange(N_DP * per_device) == forced, longest, lengths).astype(jnp.int32)


def draw_res_len(key, part):
    return skewed_lengths(key, 6, REQ, RB * BLK)


def draw_mig_len(key, part):
    return skewed_lengths(key, 8, 1, MB * BLK)


def arrival_plan(key):
    seeded = jax.random.fold_in(key, 11)
    half_count = N_DP // 2
    spread = jax.random.randint(jax.random.fold_in(seeded, 1), (half_count,), 0, OUTB)
    forced = jax.random.randint(jax.random.fold_in(seeded, 2), (), 0, half_count)
    spread = jnp.where(jnp.arange(half_count) == forced, OUTB - 1, spread)
    counts = jnp.concatenate([OUTB + spread, OUTB - spread]).astype(jnp.int32)
    owner_order = jax.random.permutation(jax.random.fold_in(seeded, 3), N_DP).astype(jnp.int32)
    starts = jnp.cumsum(counts) - counts
    positions = jnp.arange(N_DP * OUTB, dtype=jnp.int32)
    segment = jnp.sum((starts[None, :] <= positions[:, None]).astype(jnp.int32), axis=1) - 1
    owners = owner_order[segment]
    within = positions - starts[segment]
    source = positions % N_DP
    pair_slot = within // N_DP
    row_keys = jax.random.split(jax.random.fold_in(seeded, 4), N_DP)
    shuffles = jax.vmap(lambda row_key: jax.random.permutation(row_key, OUTB))(row_keys).astype(jnp.int32)
    blocks = shuffles[source, positions // N_DP]
    send_rows = jnp.full((N_DP, N_DP * CAP), -1, jnp.int32).at[source, owners * CAP + pair_slot].set(blocks)
    listed = jnp.zeros((N_DP, ARRB), jnp.int32).at[owners, within].set(source * CAP + pair_slot)
    totals = jnp.zeros((N_DP,), jnp.int32).at[owner_order].set(counts)
    return (send_rows.reshape(-1), listed.reshape(-1), totals)


def draw_send_table(key, part):
    return arrival_plan(key)[0]


def draw_arr_index(key, part):
    return arrival_plan(key)[1]


def draw_arr_count(key, part):
    return arrival_plan(key)[2]


def draw_mig_bit(key, part):
    scores = jax.random.randint(jax.random.fold_in(key, 23), (N_DP, LOGDP), 1, 1 << 20)
    levels = jnp.arange(LOGDP, dtype=jnp.int32)

    def visit_device(device, chosen_bits):
        partners = jnp.bitwise_xor(device, jnp.left_shift(jnp.int32(1), levels))
        unpaired = (chosen_bits[partners] < 0) & (chosen_bits[device] < 0)
        ranking = jnp.where(unpaired, scores[device], 0)
        ranking = jnp.where((device == 0) & (levels == LOGDP - 1), 1 << 21, ranking)
        best_bit = jnp.argmax(ranking).astype(jnp.int32)
        chosen = jnp.max(ranking) > 0
        updated = chosen_bits.at[device].set(best_bit).at[partners[best_bit]].set(best_bit)
        return jnp.where(chosen, updated, chosen_bits)
    return lax.fori_loop(0, N_DP, visit_device, jnp.full((N_DP,), -1, jnp.int32))


def query_parts(key):
    seeded = jax.random.fold_in(key, 31)
    row_count = N_DP * (REQ + 2)
    fresh = jnp.clip(jax.random.normal(jax.random.fold_in(seeded, 4), (row_count, STEPS, DL + DR), jnp.float32), -6.0, 6.0)
    queries = jnp.clip(jax.random.normal(jax.random.fold_in(seeded, 5), (row_count, STEPS, H, DL), jnp.float32), -6.0, 6.0)
    return (fresh, queries)


def draw_q_lat(key, part):
    return query_parts(key)[1].astype(jnp.bfloat16)


def draw_new_kv(key, part):
    return query_parts(key)[0].astype(jnp.bfloat16)


def place_ends(values, own_key, smallest, high):
    index_at = [jax.random.randint(jax.random.fold_in(own_key, axis), (), 0, length) for axis, length in enumerate(values.shape)]
    main_axis = values.shape.index(max(values.shape))
    beside = index_at[:main_axis] + [(index_at[main_axis] + 1) % values.shape[main_axis]] + index_at[main_axis + 1:]
    return values.at[tuple(index_at)].set(smallest).at[tuple(beside)].set(high)


def block_levels(own_key, dims, cuts, least, high):
    loudness = 1.0
    for position, parts in cuts:
        heights = jax.random.uniform(jax.random.fold_in(jax.random.fold_in(own_key, 6), position), (parts,), jnp.float32, least / len(cuts), high / len(cuts))
        loudness = loudness * jnp.repeat(jnp.exp(heights), dims[position] // parts).reshape((-1,) + (1,) * (len(dims) - 1 - position))
    return loudness


def noise(own_key, shape, scale, most, cuts=(), held_as=jnp.bfloat16):
    factor_of = block_levels(own_key, shape, cuts, -0.22, 0.18) if cuts else 1.0
    values = jax.random.normal(own_key, shape, jnp.float32) * scale * factor_of
    return jnp.minimum(jnp.maximum(values, -most), most).astype(held_as)


def setup_inputs(seed: int = 0, part: int = 0) -> dict:
    key_of = jax.random.split(jax.random.key(seed), 18)
    own_keys = jax.random.split(jax.random.fold_in(key_of[17], part), 18)
    res_lat = noise(own_keys[0], (N_DP * RESB, BLK, DL), 1.0, 6.0, ((0, 16),))
    res_rope = noise(own_keys[1], (N_DP * RESB, DR, BLK), 1.0, 6.0, ((0, 16),))
    res_table = jax.vmap(lambda own: jax.random.permutation(own, RESB))(jax.random.split(own_keys[2], N_DP)).reshape((N_DP, RESB)).astype(jnp.int32)
    res_len = draw_res_len(jax.random.fold_in(jax.random.fold_in(key_of[17], part), 71), part)
    out_lat = noise(own_keys[4], (N_DP * OUTB, BLK, DL), 1.0, 6.0, ((0, 16),))
    out_rope = noise(own_keys[5], (N_DP * OUTB, DR, BLK), 1.0, 6.0, ((0, 16),))
    out_fill = place_ends(jax.random.randint(own_keys[6], (N_DP * OUTB,), 1, BLK + 1), jax.random.fold_in(own_keys[6], 1), 1, BLK).astype(jnp.int32)
    send_table = draw_send_table(jax.random.fold_in(jax.random.fold_in(key_of[17], part), 71), part)
    arr_index = draw_arr_index(jax.random.fold_in(jax.random.fold_in(key_of[17], part), 71), part)
    arr_count = draw_arr_count(jax.random.fold_in(jax.random.fold_in(key_of[17], part), 71), part)
    mig_lat = noise(own_keys[10], (N_DP * MB, BLK, DL), 1.0, 6.0, ((0, 16),))
    mig_rope = noise(own_keys[11], (N_DP * MB, DR, BLK), 1.0, 6.0, ((0, 16),))
    mig_len = draw_mig_len(jax.random.fold_in(jax.random.fold_in(key_of[17], part), 71), part)
    mig_bit = draw_mig_bit(jax.random.fold_in(jax.random.fold_in(key_of[17], part), 71), part)
    q_lat = draw_q_lat(jax.random.fold_in(jax.random.fold_in(key_of[17], part), 71), part)
    q_rope = noise(own_keys[15], (N_DP * (REQ + 2), STEPS, DR, H), 1.0, 6.0, ((0, 16),))
    new_kv = draw_new_kv(jax.random.fold_in(jax.random.fold_in(key_of[17], part), 71), part)
    return dict(res_lat=res_lat, res_rope=res_rope, res_table=res_table, res_len=res_len, out_lat=out_lat, out_rope=out_rope, out_fill=out_fill, send_table=send_table, arr_index=arr_index, arr_count=arr_count, mig_lat=mig_lat, mig_rope=mig_rope, mig_len=mig_len, mig_bit=mig_bit, q_lat=q_lat, q_rope=q_rope, new_kv=new_kv)


score_scale = 192.0 ** -0.5


def attend(q_lat, q_rope, new_kv, key_blocks, rope_blocks, usable):
    latent = key_blocks.shape[2]
    new_lat = new_kv[:, :latent].astype(jnp.float32)
    new_rope = new_kv[:, latent:].astype(jnp.float32)
    query_lat = q_lat.astype(jnp.float32)
    query_rope = q_rope.astype(jnp.float32)
    key_lat = key_blocks.astype(jnp.float32)
    cache_scores = (jnp.einsum("thd,nkd->thnk", query_lat, key_lat)
                    + jnp.einsum("tdh,ndk->thnk", query_rope, rope_blocks.astype(jnp.float32))) * score_scale
    cache_scores = jnp.where(usable[None, None], cache_scores, -jnp.inf)
    new_scores = (jnp.einsum("thd,ud->thu", query_lat, new_lat)
                  + jnp.einsum("tdh,ud->thu", query_rope, new_rope)) * score_scale
    step_count = new_kv.shape[0]
    causal = jnp.arange(step_count)[None, :] <= jnp.arange(step_count)[:, None]
    new_scores = jnp.where(causal[:, None, :], new_scores, -jnp.inf)
    highest = jnp.maximum(jnp.max(cache_scores, axis=(2, 3)), jnp.max(new_scores, axis=2))
    cache_w = jnp.exp(cache_scores - highest[:, :, None, None])
    new_w = jnp.exp(new_scores - highest[:, :, None])
    weight_sum = jnp.sum(cache_w, axis=(2, 3)) + jnp.sum(new_w, axis=2)
    cache_round = lax.optimization_barrier(cache_w.astype(jnp.bfloat16)).astype(jnp.float32)
    new_round = lax.optimization_barrier(new_w.astype(jnp.bfloat16)).astype(jnp.float32)
    combined = jnp.einsum("thnk,nkd->thd", cache_round, key_lat) + jnp.einsum("thu,ud->thd", new_round, new_lat)
    return (combined / weight_sum[:, :, None]).astype(jnp.bfloat16)


def reference(res_lat, res_rope, res_table, res_len, out_lat, out_rope, out_fill, send_table, arr_index, arr_count,
              mig_lat, mig_rope, mig_len, mig_bit, q_lat, q_rope, new_kv):
    slots = REQ + 2
    query_lat = q_lat.reshape(N_DP, slots, STEPS, H, DL)
    query_rope = q_rope.reshape(N_DP, slots, STEPS, DR, H)
    fresh_keys = new_kv.reshape(N_DP, slots, STEPS, DL + DR)
    res_lat_dev = res_lat.reshape(N_DP, RESB, BLK, DL)
    res_rope_dev = res_rope.reshape(N_DP, RESB, DR, BLK)
    tables = res_table.reshape(N_DP, REQ, RB)
    lengths = res_len.reshape(N_DP, REQ)
    out_lat_dev = out_lat.reshape(N_DP, OUTB, BLK, DL)
    out_rope_dev = out_rope.reshape(N_DP, OUTB, DR, BLK)
    fills = out_fill.reshape(N_DP, OUTB)
    sends = send_table.reshape(N_DP, N_DP * CAP)
    arrivals = arr_index.reshape(N_DP, ARRB)
    mig_lat_dev = mig_lat.reshape(N_DP, MB, BLK, DL)
    mig_rope_dev = mig_rope.reshape(N_DP, MB, DR, BLK)
    token_pos = jnp.arange(BLK, dtype=jnp.int32)

    def one_device(device):
        def resident(request):
            indices = tables[device, request]
            usable = (jnp.arange(RB * BLK, dtype=jnp.int32) < lengths[device, request]).reshape(RB, BLK)
            return attend(query_lat[device, request], query_rope[device, request], fresh_keys[device, request],
                          res_lat_dev[device][indices], res_rope_dev[device][indices], usable)

        resident_out = lax.map(resident, jnp.arange(REQ, dtype=jnp.int32))
        received = arrivals[device]
        source = received // CAP
        blocks = jnp.maximum(sends[source, device * CAP + received % CAP], 0)
        block_fill = fills[source, blocks]
        usable = (jnp.arange(ARRB, dtype=jnp.int32) < arr_count[device])[:, None] & (token_pos[None, :] < block_fill[:, None])
        arrival_out = attend(query_lat[device, REQ], query_rope[device, REQ], fresh_keys[device, REQ],
                             out_lat_dev[source, blocks], out_rope_dev[source, blocks], usable)
        partner_bit = mig_bit[device]
        partner = jnp.where(partner_bit >= 0,
                            jnp.bitwise_xor(device, jnp.left_shift(jnp.int32(1), jnp.maximum(partner_bit, 0))),
                            device).astype(jnp.int32)
        usable = (jnp.arange(MB * BLK, dtype=jnp.int32) < mig_len[partner]).reshape(MB, BLK)
        moved_out = attend(query_lat[device, REQ + 1], query_rope[device, REQ + 1], fresh_keys[device, REQ + 1],
                           mig_lat_dev[partner], mig_rope_dev[partner], usable)
        return jnp.concatenate([resident_out, arrival_out[None], moved_out[None]], axis=0)

    result = lax.map(one_device, jnp.arange(N_DP, dtype=jnp.int32))
    return result.reshape(N_DP * slots, STEPS, H, DL)
```

```python
import functools

import jax
import jax.numpy as jnp
from jax import lax
from jax.experimental import pallas as pl
from jax.experimental.pallas import tpu as pltpu
from jax.sharding import PartitionSpec as P

score_scale = 192.0 ** (-0.5)
FILL_ROWS = 16
LAST = (((1,), (1,)), ((), ()))
PLAIN = (((1,), (0,)), ((), ()))


def dot(a, b, dims):
    return lax.dot_general(a, b, dims, preferred_element_type=jnp.float32)


def attend_kernel(
    by_fill, table_ref, count_ref, len_ref, q_lat, q_rope, new, lat, rope, out, qr, scores, total
):
    steps, heads, latent = q_lat.shape
    rows = steps * heads
    width = q_rope.shape[1]
    block = lat.shape[1]
    for t in range(steps):
        qr[t * heads : (t + 1) * heads, :] = q_rope[t].astype(jnp.float32).T.astype(jnp.bfloat16)
    query = q_lat[...].reshape(rows, latent)
    query_r = qr[...]
    count = count_ref[0]
    length = len_ref[0]
    lane = lax.broadcasted_iota(jnp.int32, (1, block), 1)

    def usable(i, b):
        if by_fill:
            fill = rope[b][width : width + 1, :].astype(jnp.float32)
            return (lane.astype(jnp.float32) < fill) & (i < count)
        return lane + i * block < length

    def score(j, highest):
        for half in range(2):
            i = 2 * j + half
            b = table_ref[i]
            s = dot(query, lat[b], LAST) + dot(query_r, rope[b][:width, :], PLAIN)
            s = jnp.where(usable(i, b), s * score_scale, -jnp.inf)
            scores[i] = s
            highest = jnp.maximum(highest, s)
        return highest

    pairs = (count + 1) // 2
    highest = lax.fori_loop(0, pairs, score, jnp.full((rows, block), -jnp.inf, jnp.float32))
    fresh = new[...]
    ns = dot(query, fresh[:, :latent], LAST) + dot(query_r, fresh[:, latent:], LAST)
    column = lax.broadcasted_iota(jnp.int32, ns.shape, 1)
    step_of = lax.broadcasted_iota(jnp.int32, ns.shape, 0) // heads
    ns = jnp.where(column <= step_of, ns * score_scale, -jnp.inf)
    top = jnp.maximum(
        jnp.max(highest, axis=1, keepdims=True), jnp.max(ns, axis=1, keepdims=True)
    )
    nw = jnp.exp(ns - top)
    total[...] = dot(nw.astype(jnp.bfloat16), fresh[:, :latent], PLAIN)

    def mix(j, sums):
        acc = None
        for half in range(2):
            i = 2 * j + half
            w = jnp.exp(scores[i] - top)
            sums = sums + w
            part = dot(w.astype(jnp.bfloat16), lat[table_ref[i]], PLAIN)
            acc = part if acc is None else acc + part
        total[...] += acc
        return sums

    sums = lax.fori_loop(0, pairs, mix, jnp.zeros((rows, block), jnp.float32))
    weight_sum = jnp.sum(sums, axis=1, keepdims=True) + jnp.sum(nw, axis=1, keepdims=True)
    out[...] = (total[...] / weight_sum).astype(jnp.bfloat16).reshape(steps, heads, latent)


def attend(table, count, length, q_lat, q_rope, new, lat, rope, by_fill):
    steps, heads, latent = q_lat.shape
    rows = steps * heads
    blocks, block = lat.shape[:2]
    listed = table.shape[0] + table.shape[0] % 2
    table = jnp.pad(table, (0, listed - table.shape[0]))
    smem = pl.BlockSpec(memory_space=pltpu.SMEM)
    vmem = pl.BlockSpec(memory_space=pltpu.VMEM)
    flops = 2 * rows * listed * block * (2 * latent + q_rope.shape[1])
    return pl.pallas_call(
        functools.partial(attend_kernel, by_fill),
        out_shape=jax.ShapeDtypeStruct(q_lat.shape, jnp.bfloat16),
        in_specs=[smem] * 3 + [vmem] * 5,
        out_specs=vmem,
        scratch_shapes=[
            pltpu.VMEM((rows, q_rope.shape[1]), jnp.bfloat16),
            pltpu.VMEM((listed, rows, block), jnp.float32),
            pltpu.VMEM((rows, latent), jnp.float32),
        ],
        compiler_params=pltpu.CompilerParams(vmem_limit_bytes=40 * 2**20),
        cost_estimate=pl.CostEstimate(
            flops=flops, bytes_accessed=lat.size * 2 + q_lat.size * 4, transcendentals=rows * listed * block
        ),
    )(table, count, length, q_lat, q_rope, new, lat, rope)


def exchange(bit_level, values):
    size = lax.axis_size("dp")
    route = [(low, low ^ (1 << bit_level)) for low in range(size)]
    return jax.tree.map(lambda value: lax.ppermute(value, "dp", route), values)


def swap(bit, values):
    levels = lax.axis_size("dp").bit_length() - 1
    branches = [lambda v: v] + [functools.partial(exchange, level) for level in range(levels)]
    return lax.switch(bit + 1, branches, values)


def shards(
    res_lat,
    res_rope,
    res_table,
    res_len,
    out_lat,
    out_rope,
    out_fill,
    send_table,
    arr_index,
    arr_count,
    mig_lat,
    mig_rope,
    mig_len,
    mig_bit,
    q_lat,
    q_rope,
    new_kv,
):
    block_len = res_lat.shape[1]
    requests = res_len.shape[0]
    steps = new_kv.shape[1]
    new = jnp.pad(new_kv, ((0, 0), (0, FILL_ROWS - steps), (0, 0)))

    picked = jnp.maximum(send_table, 0)
    fill = jnp.where(send_table >= 0, out_fill[picked], 0).astype(jnp.bfloat16)
    fill_rows = jnp.broadcast_to(fill[:, None, None], (fill.shape[0], FILL_ROWS, block_len))
    got_lat = lax.all_to_all(out_lat[picked], "dp", split_axis=0, concat_axis=0, tiled=True)
    got_rope = lax.all_to_all(
        jnp.concatenate([out_rope[picked], fill_rows], axis=1),
        "dp", split_axis=0, concat_axis=0, tiled=True,
    )

    moved = requests + 1
    visitor = swap(mig_bit[0], (q_lat[moved], q_rope[moved], new[moved]))
    mig_table = jnp.arange(mig_lat.shape[0], dtype=jnp.int32)
    mig_count = (mig_len + block_len - 1) // block_len
    computed = attend(
        mig_table, mig_count, mig_len, *visitor, mig_lat, mig_rope, False
    )
    moved_out = swap(mig_bit[0], computed)

    outs = []
    for r in range(requests):
        length = res_len[r : r + 1]
        outs.append(
            attend(
                res_table[r], (length + block_len - 1) // block_len, length,
                q_lat[r], q_rope[r], new[r], res_lat, res_rope, False,
            )
        )
    arrival_out = attend(
        arr_index, arr_count, arr_count, q_lat[requests], q_rope[requests], new[requests],
        got_lat, got_rope, True,
    )
    return jnp.stack(outs + [arrival_out, moved_out])


def solution(mesh):
    both = ("groups", "dp")
    ranks = (3, 3, 2, 1, 3, 3, 1, 1, 1, 1, 3, 3, 1, 1, 4, 4, 3)
    return jax.shard_map(
        shards,
        mesh=mesh,
        in_specs=tuple(P(both, *([None] * (rank - 1))) for rank in ranks),
        out_specs=P(both, None, None, None),
        check_vma=False,
    )
```

```python
import functools

import jax
import jax.numpy as jnp
from jax import lax
from jax.experimental import pallas as pl
from jax.experimental.pallas import tpu as pltpu
from jax.sharding import PartitionSpec as P

score_scale = 192.0 ** (-0.5)
EXTRA = 8
FRESH = 16
LAST = (((1,), (1,)), ((), ()))
PLAIN = (((1,), (0,)), ((), ()))
VMEM_BYTES = 56 * 2**20


def dot(a, b, dims):
    return lax.dot_general(a, b, dims, preferred_element_type=jnp.float32)


def fold(rope, latent):
    parts = latent // rope.shape[1]
    each = rope.shape[0] // parts
    return jnp.concatenate([rope[p * each : (p + 1) * each] for p in range(parts)], axis=1)


def unfold(folded, width):
    parts = folded.shape[1] // width
    return jnp.concatenate([folded[:, p * width : (p + 1) * width] for p in range(parts)], axis=0)


def pack_kernel(table, fills, lat, rope, q_lat, q_rope, new, sent, payload):
    slots, latent = sent.shape[0], sent.shape[2]
    block = lat.shape[1]
    folded = rope.shape[1] * rope.shape[2] // latent
    top = block + folded

    def slot(s, carry):
        b = table[s]

        @pl.when(b >= 0)
        def _():
            sent[s, :block, :] = lat[b]
            sent[s, block:top, :] = fold(rope[b], latent)
            fill = fills[b].astype(jnp.float32)
            sent[s, top:, :] = jnp.full((EXTRA, latent), fill, jnp.float32).astype(jnp.bfloat16)

        return carry

    lax.fori_loop(0, slots, slot, 0)
    steps, heads = q_lat.shape[1:3]
    fresh = new[0].astype(jnp.float32)
    width = fresh.shape[1] - latent
    for t in range(steps):
        payload[t, :heads, :] = q_lat[0, t]
        payload[t, heads : heads + folded, :] = fold(q_rope[0, t], latent)
        rope_row = jnp.concatenate(
            [fresh[t : t + 1, latent:], jnp.zeros((1, latent - width), jnp.float32)], axis=1
        )
        payload[t, heads + folded :, :] = jnp.concatenate(
            [fresh[t : t + 1, :latent], rope_row, jnp.zeros((EXTRA - 2, latent), jnp.float32)], axis=0
        ).astype(jnp.bfloat16)


def pick(slot, array):
    rest = array.shape[1:]
    return pl.BlockSpec((1,) + rest, lambda i: (slot,) + (0,) * len(rest))


def whole(array):
    return pl.BlockSpec(array.shape, lambda i: (0,) * len(array.shape))


def pack(send_table, out_fill, out_lat, out_rope, q_lat, q_rope, new_kv, moved):
    block, latent = out_lat.shape[1:]
    steps, heads = q_lat.shape[1:3]
    folded = out_rope.shape[1] * out_rope.shape[2] // latent
    smem = pl.BlockSpec(memory_space=pltpu.SMEM)
    shapes = (
        jax.ShapeDtypeStruct((send_table.shape[0], block + folded + EXTRA, latent), jnp.bfloat16),
        jax.ShapeDtypeStruct((steps, heads + folded + EXTRA, latent), jnp.bfloat16),
    )
    return pl.pallas_call(
        pack_kernel,
        grid=(1,),
        out_shape=shapes,
        in_specs=[smem, smem, whole(out_lat), whole(out_rope)]
        + [pick(moved, a) for a in (q_lat, q_rope, new_kv)],
        out_specs=tuple(whole(s) for s in shapes),
        compiler_params=pltpu.CompilerParams(vmem_limit_bytes=VMEM_BYTES),
    )(send_table, out_fill, out_lat, out_rope, q_lat, q_rope, new_kv)


def attention(
    by_fill, table, count, length, latv, ropev, sem, copies, query, query_r, fresh, scores, total
):
    rows, latent = query.shape
    width = query_r.shape[1]
    block = scores.shape[2] // 2
    lane = lax.broadcasted_iota(jnp.int32, (1, block), 1)
    folded = width * block // latent

    def begin(i, carry):
        for copy in copies(i, table[i]):
            copy.start()
        return carry

    lax.fori_loop(0, count, begin, 0)
    pairs = (count + 1) // 2

    @pl.when(count % 2 == 1)
    def _():
        latv[count] = jnp.zeros(latv.shape[1:], latv.dtype)
        if ropev is not None:
            ropev[count] = jnp.zeros(ropev.shape[1:], ropev.dtype)

    def score(j, highest):
        ropes, masks = [], []
        for half in range(2):
            i = 2 * j + half

            @pl.when(i < count)
            def _():
                for copy in copies(i, table[i]):
                    copy.wait()

        for half in range(2):
            i = 2 * j + half
            if by_fill:
                ropes.append(unfold(latv[i, block : block + folded, :], block))
                fill = latv[i, block + folded : block + folded + EXTRA, :block][:1].astype(jnp.float32)
                masks.append(jnp.where(i < count, fill, 0.0))
            else:
                ropes.append(ropev[i])
                masks.append(jnp.full((1, block), length - i * block, jnp.int32).astype(jnp.float32))
        keys = latv[pl.ds(2 * j, 2)][:, :block, :].reshape(2 * block, latent)
        s = dot(query, keys, LAST) + dot(query_r, jnp.concatenate(ropes, axis=1), PLAIN)
        lanes = lane.astype(jnp.float32)
        usable = jnp.concatenate([jnp.where(lanes < m, 0.0, -jnp.inf) for m in masks], axis=1)
        s = s * score_scale + usable
        scores[j] = s
        return jnp.maximum(highest, jnp.maximum(s[:, :block], s[:, block:]))

    highest = lax.fori_loop(0, pairs, score, jnp.full((rows, block), -jnp.inf, jnp.float32))
    ns = dot(query, fresh[:, :latent], LAST) + dot(query_r, fresh[:, latent:], LAST)
    column = lax.broadcasted_iota(jnp.int32, ns.shape, 1)
    step_of = lax.broadcasted_iota(jnp.int32, ns.shape, 0) // total[1]
    ns = jnp.where(column <= step_of, ns * score_scale, -jnp.inf)
    top = jnp.maximum(
        jnp.max(highest, axis=1, keepdims=True), jnp.max(ns, axis=1, keepdims=True)
    )
    nw = jnp.exp(ns - top)
    acc = total[0]
    acc[...] = dot(nw.astype(jnp.bfloat16), fresh[:, :latent], PLAIN)

    def mix(j, sums):
        w = jnp.exp(scores[j] - top)
        keys = latv[pl.ds(2 * j, 2)][:, :block, :].reshape(2 * block, latent)
        acc[...] += dot(w.astype(jnp.bfloat16), keys, PLAIN)
        return sums + (w[:, :block] + w[:, block:])

    sums = lax.fori_loop(0, pairs, mix, jnp.zeros((rows, block), jnp.float32))
    weight_sum = jnp.sum(sums, axis=1, keepdims=True) + jnp.sum(nw, axis=1, keepdims=True)
    return (acc[...] / weight_sum).astype(jnp.bfloat16)


def turned(rope):
    return rope.astype(jnp.float32).T.astype(jnp.bfloat16)


def owned_kernel(by_fill, slot, has_base, moved, table, count, length, q_lat, q_rope, new, *refs):
    refs = list(refs)
    lat = refs.pop(0)
    rope = None if by_fill else refs.pop(0)
    if has_base:
        refs.pop(0)
    result = refs.pop(0) if moved is not None else None
    out, latv = refs.pop(0), refs.pop(0)
    ropev = None if by_fill else refs.pop(0)
    scores, acc, done, sem, out_sem = refs
    if moved is not None:
        extra = pltpu.make_async_copy(result, out.at[moved], out_sem.at[1])
        extra.start()

    def copies(i, b):
        made = [pltpu.make_async_copy(lat.at[b], latv.at[i], sem.at[0, i])]
        if not by_fill:
            made.append(pltpu.make_async_copy(rope.at[b], ropev.at[i], sem.at[1, i]))
        return made

    steps, heads, latent = q_lat.shape[1:]
    query = q_lat[0].reshape(steps * heads, latent)
    query_r = jnp.concatenate([turned(q_rope[0, t]) for t in range(steps)], axis=0)
    fresh = new[0].astype(jnp.float32)
    fresh = jnp.concatenate(
        [fresh, jnp.zeros((FRESH - steps, fresh.shape[1]), jnp.float32)], axis=0
    ).astype(jnp.bfloat16)
    value = attention(
        by_fill, table, count[0], length[0], latv, ropev, sem, copies, query, query_r, fresh, scores,
        (acc, heads),
    )
    done[...] = value.reshape(steps, heads, latent)
    back = pltpu.make_async_copy(done, out.at[slot], out_sem.at[0])
    back.start()
    back.wait()
    if moved is not None:
        extra.wait()


def owned(slot, table, count, length, q_lat, q_rope, new_kv, lat, rope, base=None, result=None, moved=None):
    by_fill = rope is None
    steps, heads, latent = q_lat.shape[1:]
    rows = steps * heads
    width, block = q_rope.shape[2], heads if by_fill else lat.shape[1]
    if by_fill:
        block = lat.shape[1] - EXTRA
        block = block * latent // (latent + width)
    listed = table.shape[0] + table.shape[0] % 2
    smem = pl.BlockSpec(memory_space=pltpu.SMEM)
    far = pl.BlockSpec(memory_space=pl.ANY)
    operands = [table, count, length, q_lat, q_rope, new_kv, lat]
    specs = [smem] * 3 + [pick(slot, a) for a in (q_lat, q_rope, new_kv)] + [far]
    scratch = [pltpu.VMEM((listed,) + lat.shape[1:], jnp.bfloat16)]
    if not by_fill:
        operands.append(rope)
        specs.append(far)
        scratch.append(pltpu.VMEM((listed,) + rope.shape[1:], jnp.bfloat16))
    aliases = {}
    if base is not None:
        aliases = {len(operands): 0}
        operands.append(base)
        specs.append(far)
    if result is not None:
        operands.append(result)
        specs.append(far)
    return pl.pallas_call(
        functools.partial(owned_kernel, by_fill, slot, base is not None, moved),
        grid=(1,),
        out_shape=jax.ShapeDtypeStruct(q_lat.shape, jnp.bfloat16),
        in_specs=specs,
        out_specs=far,
        scratch_shapes=scratch
        + [
            pltpu.VMEM((listed // 2, rows, 2 * block), jnp.float32),
            pltpu.VMEM((rows, latent), jnp.float32),
            pltpu.VMEM((steps, heads, latent), jnp.bfloat16),
            pltpu.SemaphoreType.DMA((2, listed)),
            pltpu.SemaphoreType.DMA((2,)),
        ],
        input_output_aliases=aliases,
        compiler_params=pltpu.CompilerParams(vmem_limit_bytes=VMEM_BYTES),
        cost_estimate=pl.CostEstimate(
            flops=2 * rows * listed * block * (2 * latent + width),
            bytes_accessed=lat.size * 2 + rows * latent * 4,
            transcendentals=rows * listed * block,
        ),
    )(*operands)


def visitor_kernel(width, length, payload, lat, rope, out, latv, ropev, scores, acc, sem):
    steps, heads, latent = out.shape
    block = lat.shape[1]
    folded = width * heads // latent
    top = heads + folded

    def copies(i, b):
        return [
            pltpu.make_async_copy(lat.at[b], latv.at[i], sem.at[0, i]),
            pltpu.make_async_copy(rope.at[b], ropev.at[i], sem.at[1, i]),
        ]

    query = payload[:, :heads, :].reshape(steps * heads, latent)
    query_r = jnp.concatenate(
        [turned(unfold(payload[t, heads:top, :], heads)) for t in range(steps)], axis=0
    )
    tails = [payload[t, top:, :].astype(jnp.float32) for t in range(steps)]
    fresh = jnp.concatenate(
        [jnp.concatenate([tail[0:1], tail[1:2, :width]], axis=1) for tail in tails]
        + [jnp.zeros((FRESH - steps, latent + width), jnp.float32)],
        axis=0,
    ).astype(jnp.bfloat16)
    count = (length[0] + block - 1) // block
    value = attention(
        False, lambda_table, count, length[0], latv, ropev, sem, copies, query, query_r, fresh, scores,
        (acc, heads),
    )
    out[...] = value.reshape(steps, heads, latent)


class Straight:
    def __getitem__(self, i):
        return i


lambda_table = Straight()


def visited(length, payload, lat, rope, heads):
    steps, latent = payload.shape[0], payload.shape[2]
    rows = steps * heads
    blocks, width, block = rope.shape
    listed = blocks + blocks % 2
    far = pl.BlockSpec(memory_space=pl.ANY)
    shape = jax.ShapeDtypeStruct((steps, heads, latent), jnp.bfloat16)
    return pl.pallas_call(
        functools.partial(visitor_kernel, width),
        grid=(1,),
        out_shape=shape,
        in_specs=[pl.BlockSpec(memory_space=pltpu.SMEM), whole(payload), far, far],
        out_specs=whole(shape),
        scratch_shapes=[
            pltpu.VMEM((listed,) + lat.shape[1:], jnp.bfloat16),
            pltpu.VMEM((listed,) + rope.shape[1:], jnp.bfloat16),
            pltpu.VMEM((listed // 2, rows, 2 * block), jnp.float32),
            pltpu.VMEM((rows, latent), jnp.float32),
            pltpu.SemaphoreType.DMA((2, listed)),
        ],
        compiler_params=pltpu.CompilerParams(vmem_limit_bytes=VMEM_BYTES),
        cost_estimate=pl.CostEstimate(
            flops=2 * rows * listed * block * (2 * latent + width),
            bytes_accessed=lat.size * 2 + rows * latent * 4,
            transcendentals=rows * listed * block,
        ),
    )(length, payload, lat, rope)


def exchange(bit_level, value):
    size = lax.axis_size("dp")
    route = [(low, low ^ (1 << bit_level)) for low in range(size)]
    return lax.ppermute(value, "dp", route)


def swap(bit, value):
    levels = lax.axis_size("dp").bit_length() - 1
    branches = [lambda v: v] + [functools.partial(exchange, level) for level in range(levels)]
    return lax.switch(bit + 1, branches, value)


def shards(
    res_lat,
    res_rope,
    res_table,
    res_len,
    out_lat,
    out_rope,
    out_fill,
    send_table,
    arr_index,
    arr_count,
    mig_lat,
    mig_rope,
    mig_len,
    mig_bit,
    q_lat,
    q_rope,
    new_kv,
):
    block_len = res_lat.shape[1]
    requests = res_len.shape[0]
    heads = q_lat.shape[2]
    moved = requests + 1

    sent, payload = pack(send_table, out_fill, out_lat, out_rope, q_lat, q_rope, new_kv, moved)
    visitor = swap(mig_bit[0], payload)
    sent, visitor = lax.optimization_barrier((sent, visitor))
    got = lax.all_to_all(sent, "dp", split_axis=0, concat_axis=0, tiled=True)

    computed = visited(mig_len, visitor, mig_lat, mig_rope, heads)
    out = None
    for r in range(requests):
        length = res_len[r : r + 1]
        out = owned(
            r, res_table[r], (length + block_len - 1) // block_len, length, q_lat, q_rope, new_kv,
            res_lat, res_rope, base=out,
        )
    computed, out = lax.optimization_barrier((computed, out))
    moved_out = swap(mig_bit[0], computed)
    return owned(
        requests, arr_index, arr_count, arr_count, q_lat, q_rope, new_kv, got, None,
        base=out, result=moved_out, moved=moved,
    )


def solution(mesh):
    both = ("groups", "dp")
    ranks = (3, 3, 2, 1, 3, 3, 1, 1, 1, 1, 3, 3, 1, 1, 4, 4, 3)
    return jax.shard_map(
        shards,
        mesh=mesh,
        in_specs=tuple(P(both, *([None] * (rank - 1))) for rank in ranks),
        out_specs=P(both, None, None, None),
        check_vma=False,
    )
```

```python
import functools

import jax
import jax.numpy as jnp
from jax import lax
from jax.experimental import pallas as pl
from jax.experimental.pallas import tpu as pltpu
from jax.sharding import PartitionSpec as P

score_scale = 192.0 ** (-0.5)
EXTRA = 8
FRESH = 16
LAST = (((1,), (1,)), ((), ()))
PLAIN = (((1,), (0,)), ((), ()))
VMEM_BYTES = 56 * 2**20


def dot(a, b, dims):
    return lax.dot_general(a, b, dims, preferred_element_type=jnp.float32)


def fold(rope, latent):
    parts = latent // rope.shape[1]
    each = rope.shape[0] // parts
    return jnp.concatenate([rope[p * each : (p + 1) * each] for p in range(parts)], axis=1)


def unfold(folded, width):
    parts = folded.shape[1] // width
    return jnp.concatenate([folded[:, p * width : (p + 1) * width] for p in range(parts)], axis=0)


def blocks_kernel(table, fills, lat, rope, sent):
    slots, latent = sent.shape[0], sent.shape[2]
    block = lat.shape[1]
    lane = lax.broadcasted_iota(jnp.int32, rope.shape[1:], 1)

    def slot(s, carry):
        b = table[s]

        @pl.when(b >= 0)
        def _():
            sent[s, :block, :] = lat[b]
            marked = jnp.where(lane < fills[b], rope[b].astype(jnp.float32), jnp.inf)
            sent[s, block:, :] = fold(marked.astype(jnp.bfloat16), latent)

        return carry

    lax.fori_loop(0, slots, slot, 0)


def payload_kernel(q_lat, q_rope, new, payload):
    steps, heads = q_lat.shape[1:3]
    latent = payload.shape[2]
    folded = payload.shape[1] - heads - EXTRA
    fresh = new[0].astype(jnp.float32)
    width = fresh.shape[1] - latent
    for t in range(steps):
        payload[t, :heads, :] = q_lat[0, t]
        payload[t, heads : heads + folded, :] = fold(q_rope[0, t], latent)
        rope_row = jnp.concatenate(
            [fresh[t : t + 1, latent:], jnp.zeros((1, latent - width), jnp.float32)], axis=1
        )
        payload[t, heads + folded :, :] = jnp.concatenate(
            [fresh[t : t + 1, :latent], rope_row, jnp.zeros((EXTRA - 2, latent), jnp.float32)], axis=0
        ).astype(jnp.bfloat16)


def pick(slot, array):
    rest = array.shape[1:]
    return pl.BlockSpec((1,) + rest, lambda i: (slot,) + (0,) * len(rest))


def whole(array):
    return pl.BlockSpec(array.shape, lambda i: (0,) * len(array.shape))


def pack_blocks(send_table, out_fill, out_lat, out_rope):
    block, latent = out_lat.shape[1:]
    folded = out_rope.shape[1] * out_rope.shape[2] // latent
    smem = pl.BlockSpec(memory_space=pltpu.SMEM)
    shape = jax.ShapeDtypeStruct((send_table.shape[0], block + folded, latent), jnp.bfloat16)
    return pl.pallas_call(
        blocks_kernel,
        grid=(1,),
        out_shape=shape,
        in_specs=[smem, smem, whole(out_lat), whole(out_rope)],
        out_specs=whole(shape),
        compiler_params=pltpu.CompilerParams(vmem_limit_bytes=VMEM_BYTES),
        cost_estimate=pl.CostEstimate(flops=0, bytes_accessed=shape.size * 4, transcendentals=0),
    )(send_table, out_fill, out_lat, out_rope)


def pack_payload(q_lat, q_rope, new_kv, moved):
    steps, heads, latent = q_lat.shape[1:]
    folded = q_rope.shape[2] * heads // latent
    shape = jax.ShapeDtypeStruct((steps, heads + folded + EXTRA, latent), jnp.bfloat16)
    return pl.pallas_call(
        payload_kernel,
        grid=(1,),
        out_shape=shape,
        in_specs=[pick(moved, a) for a in (q_lat, q_rope, new_kv)],
        out_specs=whole(shape),
        compiler_params=pltpu.CompilerParams(vmem_limit_bytes=VMEM_BYTES),
    )(q_lat, q_rope, new_kv)


def attention(
    by_fill, table, count, length, latv, ropev, sem, copies, query, query_r, fresh, scores, total
):
    rows, latent = query.shape
    width = query_r.shape[1]
    block = scores.shape[2] // 2
    lane = lax.broadcasted_iota(jnp.int32, (1, block), 1)

    def begin(i, carry):
        for copy in copies(i, table[i]):
            copy.start()
        return carry

    lax.fori_loop(0, count, begin, 0)
    pairs = (count + 1) // 2

    @pl.when(count % 2 == 1)
    def _():
        latv[count] = jnp.zeros(latv.shape[1:], latv.dtype)
        if ropev is not None:
            ropev[count] = jnp.zeros(ropev.shape[1:], ropev.dtype)

    def score(j, highest):
        ropes, masks = [], []
        for half in range(2):
            i = 2 * j + half

            @pl.when(i < count)
            def _():
                for copy in copies(i, table[i]):
                    copy.wait()

        for half in range(2):
            i = 2 * j + half
            if by_fill:
                carried = unfold(latv[i, block:, :], block).astype(jnp.float32)
                marked = carried < jnp.inf
                ropes.append(jnp.where(marked, carried, 0.0).astype(jnp.bfloat16))
                masks.append(jnp.where(marked[:1] & (i < count), 0.0, -jnp.inf))
            else:
                ropes.append(ropev[i])
                masks.append(jnp.where(lane + i * block < length, 0.0, -jnp.inf))
        keys = latv[pl.ds(2 * j, 2)][:, :block, :].reshape(2 * block, latent)
        s = dot(query, keys, LAST) + dot(query_r, jnp.concatenate(ropes, axis=1), PLAIN)
        s = s * score_scale + jnp.concatenate(masks, axis=1)
        scores[j] = s
        return jnp.maximum(highest, jnp.maximum(s[:, :block], s[:, block:]))

    highest = lax.fori_loop(0, pairs, score, jnp.full((rows, block), -jnp.inf, jnp.float32))
    ns = dot(query, fresh[:, :latent], LAST) + dot(query_r, fresh[:, latent:], LAST)
    column = lax.broadcasted_iota(jnp.int32, ns.shape, 1)
    step_of = lax.broadcasted_iota(jnp.int32, ns.shape, 0) // total[1]
    ns = jnp.where(column <= step_of, ns * score_scale, -jnp.inf)
    top = jnp.maximum(
        jnp.max(highest, axis=1, keepdims=True), jnp.max(ns, axis=1, keepdims=True)
    )
    nw = jnp.exp(ns - top)
    acc = total[0]
    acc[...] = dot(nw.astype(jnp.bfloat16), fresh[:, :latent], PLAIN)

    def mix(j, sums):
        w = jnp.exp(scores[j] - top)
        keys = latv[pl.ds(2 * j, 2)][:, :block, :].reshape(2 * block, latent)
        acc[...] += dot(w.astype(jnp.bfloat16), keys, PLAIN)
        return sums + (w[:, :block] + w[:, block:])

    sums = lax.fori_loop(0, pairs, mix, jnp.zeros((rows, block), jnp.float32))
    weight_sum = jnp.sum(sums, axis=1, keepdims=True) + jnp.sum(nw, axis=1, keepdims=True)
    return (acc[...] / weight_sum).astype(jnp.bfloat16)


def turned(rope):
    return rope.astype(jnp.float32).T.astype(jnp.bfloat16)


def owned_kernel(by_fill, slot, has_base, moved, table, count, length, q_lat, q_rope, new, *refs):
    refs = list(refs)
    lat = refs.pop(0)
    rope = None if by_fill else refs.pop(0)
    if has_base:
        refs.pop(0)
    result = refs.pop(0) if moved is not None else None
    out, latv = refs.pop(0), refs.pop(0)
    ropev = None if by_fill else refs.pop(0)
    scores, acc, done, sem, out_sem = refs
    if moved is not None:
        extra = pltpu.make_async_copy(result, out.at[moved], out_sem.at[1])
        extra.start()

    def copies(i, b):
        made = [pltpu.make_async_copy(lat.at[b], latv.at[i], sem.at[0, i])]
        if not by_fill:
            made.append(pltpu.make_async_copy(rope.at[b], ropev.at[i], sem.at[1, i]))
        return made

    steps, heads, latent = q_lat.shape[1:]
    query = q_lat[0].reshape(steps * heads, latent)
    query_r = jnp.concatenate([turned(q_rope[0, t]) for t in range(steps)], axis=0)
    fresh = new[0].astype(jnp.float32)
    fresh = jnp.concatenate(
        [fresh, jnp.zeros((FRESH - steps, fresh.shape[1]), jnp.float32)], axis=0
    ).astype(jnp.bfloat16)
    value = attention(
        by_fill, table, count[0], length[0], latv, ropev, sem, copies, query, query_r, fresh, scores,
        (acc, heads),
    )
    done[...] = value.reshape(steps, heads, latent)
    back = pltpu.make_async_copy(done, out.at[slot], out_sem.at[0])
    back.start()
    back.wait()
    if moved is not None:
        extra.wait()


def owned(slot, table, count, length, q_lat, q_rope, new_kv, lat, rope, base=None, result=None, moved=None):
    by_fill = rope is None
    steps, heads, latent = q_lat.shape[1:]
    rows = steps * heads
    width, block = q_rope.shape[2], heads if by_fill else lat.shape[1]
    if by_fill:
        block = lat.shape[1] * latent // (latent + width)
    listed = table.shape[0] + table.shape[0] % 2
    smem = pl.BlockSpec(memory_space=pltpu.SMEM)
    far = pl.BlockSpec(memory_space=pl.ANY)
    operands = [table, count, length, q_lat, q_rope, new_kv, lat]
    specs = [smem] * 3 + [pick(slot, a) for a in (q_lat, q_rope, new_kv)] + [far]
    scratch = [pltpu.VMEM((listed,) + lat.shape[1:], jnp.bfloat16)]
    if not by_fill:
        operands.append(rope)
        specs.append(far)
        scratch.append(pltpu.VMEM((listed,) + rope.shape[1:], jnp.bfloat16))
    aliases = {}
    if base is not None:
        aliases = {len(operands): 0}
        operands.append(base)
        specs.append(far)
    if result is not None:
        operands.append(result)
        specs.append(whole(result))
    return pl.pallas_call(
        functools.partial(owned_kernel, by_fill, slot, base is not None, moved),
        grid=(1,),
        out_shape=jax.ShapeDtypeStruct(q_lat.shape, jnp.bfloat16),
        in_specs=specs,
        out_specs=far,
        scratch_shapes=scratch
        + [
            pltpu.VMEM((listed // 2, rows, 2 * block), jnp.float32),
            pltpu.VMEM((rows, latent), jnp.float32),
            pltpu.VMEM((steps, heads, latent), jnp.bfloat16),
            pltpu.SemaphoreType.DMA((2, listed)),
            pltpu.SemaphoreType.DMA((2,)),
        ],
        input_output_aliases=aliases,
        compiler_params=pltpu.CompilerParams(vmem_limit_bytes=24 * 2**20 if by_fill else VMEM_BYTES),
        cost_estimate=pl.CostEstimate(
            flops=2 * rows * listed * block * (2 * latent + width),
            bytes_accessed=lat.size * 2 + rows * latent * 4,
            transcendentals=rows * listed * block,
        ),
    )(*operands)


def visitor_kernel(width, length, payload, lat, rope, out, latv, ropev, scores, acc, sem):
    steps, heads, latent = out.shape
    block = lat.shape[1]
    folded = width * heads // latent
    top = heads + folded

    def copies(i, b):
        return [
            pltpu.make_async_copy(lat.at[b], latv.at[i], sem.at[0, i]),
            pltpu.make_async_copy(rope.at[b], ropev.at[i], sem.at[1, i]),
        ]

    query = payload[:, :heads, :].reshape(steps * heads, latent)
    query_r = jnp.concatenate(
        [turned(unfold(payload[t, heads:top, :], heads)) for t in range(steps)], axis=0
    )
    tails = [payload[t, top:, :].astype(jnp.float32) for t in range(steps)]
    fresh = jnp.concatenate(
        [jnp.concatenate([tail[0:1], tail[1:2, :width]], axis=1) for tail in tails]
        + [jnp.zeros((FRESH - steps, latent + width), jnp.float32)],
        axis=0,
    ).astype(jnp.bfloat16)
    count = (length[0] + block - 1) // block
    value = attention(
        False, lambda_table, count, length[0], latv, ropev, sem, copies, query, query_r, fresh, scores,
        (acc, heads),
    )
    out[...] = value.reshape(steps, heads, latent)


class Straight:
    def __getitem__(self, i):
        return i


lambda_table = Straight()


def visited(length, payload, lat, rope, heads):
    steps, latent = payload.shape[0], payload.shape[2]
    rows = steps * heads
    blocks, width, block = rope.shape
    listed = blocks + blocks % 2
    far = pl.BlockSpec(memory_space=pl.ANY)
    shape = jax.ShapeDtypeStruct((steps, heads, latent), jnp.bfloat16)
    return pl.pallas_call(
        functools.partial(visitor_kernel, width),
        grid=(1,),
        out_shape=shape,
        in_specs=[pl.BlockSpec(memory_space=pltpu.SMEM), whole(payload), far, far],
        out_specs=whole(shape),
        scratch_shapes=[
            pltpu.VMEM((listed,) + lat.shape[1:], jnp.bfloat16),
            pltpu.VMEM((listed,) + rope.shape[1:], jnp.bfloat16),
            pltpu.VMEM((listed // 2, rows, 2 * block), jnp.float32),
            pltpu.VMEM((rows, latent), jnp.float32),
            pltpu.SemaphoreType.DMA((2, listed)),
        ],
        compiler_params=pltpu.CompilerParams(vmem_limit_bytes=VMEM_BYTES),
        cost_estimate=pl.CostEstimate(
            flops=2 * rows * listed * block * (2 * latent + width),
            bytes_accessed=lat.size * 2 + rows * latent * 4,
            transcendentals=rows * listed * block,
        ),
    )(length, payload, lat, rope)


def swap(bit, value, beside=None):
    size = lax.axis_size("dp")

    def branch(level, operand):
        route = [(low, low ^ (1 << max(level, 0))) for low in range(size)]
        got = operand if level < 0 else lax.ppermute(operand, "dp", route)
        return got if beside is None else (got, beside())

    levels = range(-1, size.bit_length() - 1)
    return lax.switch(bit + 1, [functools.partial(branch, level) for level in levels], value)


def shards(
    res_lat,
    res_rope,
    res_table,
    res_len,
    out_lat,
    out_rope,
    out_fill,
    send_table,
    arr_index,
    arr_count,
    mig_lat,
    mig_rope,
    mig_len,
    mig_bit,
    q_lat,
    q_rope,
    new_kv,
):
    block_len = res_lat.shape[1]
    requests = res_len.shape[0]
    heads = q_lat.shape[2]
    moved = requests + 1

    payload = pack_payload(q_lat, q_rope, new_kv, moved)
    visitor, sent = swap(
        mig_bit[0], payload, lambda: pack_blocks(send_table, out_fill, out_lat, out_rope)
    )
    sent, visitor = lax.optimization_barrier((sent, visitor))
    got = lax.all_to_all(sent, "dp", split_axis=0, concat_axis=0, tiled=True)

    computed = visited(mig_len, visitor, mig_lat, mig_rope, heads)
    out = None
    for r in range(requests):
        length = res_len[r : r + 1]
        out = owned(
            r, res_table[r], (length + block_len - 1) // block_len, length, q_lat, q_rope, new_kv,
            res_lat, res_rope, base=out,
        )
    computed, out = lax.optimization_barrier((computed, out))
    moved_out = swap(mig_bit[0], computed)
    return owned(
        requests, arr_index, arr_count, arr_count, q_lat, q_rope, new_kv, got, None,
        base=out, result=moved_out, moved=moved,
    )


def solution(mesh):
    both = ("groups", "dp")
    ranks = (3, 3, 2, 1, 3, 3, 1, 1, 1, 1, 3, 3, 1, 1, 4, 4, 3)
    return jax.shard_map(
        shards,
        mesh=mesh,
        in_specs=tuple(P(both, *([None] * (rank - 1))) for rank in ranks),
        out_specs=P(both, None, None, None),
        check_vma=False,
    )
```

```python
import functools

import jax
import jax.numpy as jnp
from jax import lax
from jax.experimental import pallas as pl
from jax.experimental.pallas import tpu as pltpu
from jax.sharding import PartitionSpec as P

score_scale = 192.0 ** (-0.5)
FRESH = 16
LAST = (((1,), (1,)), ((), ()))
PLAIN = (((1,), (0,)), ((), ()))
VMEM_BYTES = 56 * 2**20


def dot(a, b, dims):
    return lax.dot_general(a, b, dims, preferred_element_type=jnp.float32)


def fold(rope, latent):
    parts = latent // rope.shape[1]
    each = rope.shape[0] // parts
    return jnp.concatenate([rope[p * each : (p + 1) * each] for p in range(parts)], axis=1)


def unfold(folded, width):
    parts = folded.shape[1] // width
    return jnp.concatenate([folded[:, p * width : (p + 1) * width] for p in range(parts)], axis=0)


def blocks_kernel(table, fills, length, lat, rope, mig_lat, mig_rope, sent, kept):
    latent = sent.shape[2]
    block = lat.shape[1]
    lane = lax.broadcasted_iota(jnp.int32, rope.shape[1:], 1)

    def put(into, s, lat_block, rope_block, used):
        into[s, :block, :] = lat_block
        marked = jnp.where(lane < used, rope_block.astype(jnp.float32), jnp.inf)
        into[s, block:, :] = fold(marked.astype(jnp.bfloat16), latent)

    def slot(s, carry):
        b = table[s]

        @pl.when(b >= 0)
        def _():
            put(sent, s, lat[b], rope[b], fills[b])

        return carry

    def cached(i, carry):
        put(kept, i, mig_lat[i], mig_rope[i], length[0] - i * block)
        return carry

    lax.fori_loop(0, sent.shape[0], slot, 0)
    lax.fori_loop(0, (length[0] + block - 1) // block, cached, 0)


def pick(slot, array):
    rest = array.shape[1:]
    return pl.BlockSpec((1,) + rest, lambda i: (slot,) + (0,) * len(rest))


def whole(array):
    return pl.BlockSpec(array.shape, lambda i: (0,) * len(array.shape))


def pack_blocks(send_table, out_fill, mig_len, out_lat, out_rope, mig_lat, mig_rope):
    block, latent = out_lat.shape[1:]
    rows = block + out_rope.shape[1] * out_rope.shape[2] // latent
    smem = pl.BlockSpec(memory_space=pltpu.SMEM)
    shapes = tuple(
        jax.ShapeDtypeStruct((count, rows, latent), jnp.bfloat16)
        for count in (send_table.shape[0], mig_lat.shape[0])
    )
    blocks = (out_lat, out_rope, mig_lat, mig_rope)
    return pl.pallas_call(
        blocks_kernel,
        grid=(1,),
        out_shape=shapes,
        in_specs=[smem] * 3 + [whole(a) for a in blocks],
        out_specs=tuple(whole(shape) for shape in shapes),
        compiler_params=pltpu.CompilerParams(vmem_limit_bytes=VMEM_BYTES),
        cost_estimate=pl.CostEstimate(
            flops=0, bytes_accessed=sum(shape.size for shape in shapes) * 4, transcendentals=0
        ),
    )(send_table, out_fill, mig_len, *blocks)


def attention(
    by_fill, table, count, length, latv, ropev, sem, copies, query, query_r, fresh, scores, total
):
    rows, latent = query.shape
    width = query_r.shape[1]
    block = scores.shape[2] // 2
    lane = lax.broadcasted_iota(jnp.int32, (1, block), 1)

    def begin(i, carry):
        for copy in copies(i, table[i]):
            copy.start()
        return carry

    lax.fori_loop(0, count, begin, 0)
    pairs = (count + 1) // 2

    @pl.when(count % 2 == 1)
    def _():
        latv[count] = jnp.zeros(latv.shape[1:], latv.dtype)
        if ropev is not None:
            ropev[count] = jnp.zeros(ropev.shape[1:], ropev.dtype)

    def score(j, highest):
        ropes, masks = [], []
        for half in range(2):
            i = 2 * j + half

            @pl.when(i < count)
            def _():
                for copy in copies(i, table[i]):
                    copy.wait()

        for half in range(2):
            i = 2 * j + half
            if by_fill:
                carried = unfold(latv[i, block:, :], block).astype(jnp.float32)
                marked = carried < jnp.inf
                ropes.append(jnp.where(marked, carried, 0.0).astype(jnp.bfloat16))
                masks.append(jnp.where(marked[:1] & (i < count), 0.0, -jnp.inf))
            else:
                ropes.append(ropev[i])
                masks.append(jnp.where(lane + i * block < length, 0.0, -jnp.inf))
        keys = latv[pl.ds(2 * j, 2)][:, :block, :].reshape(2 * block, latent)
        s = dot(query, keys, LAST) + dot(query_r, jnp.concatenate(ropes, axis=1), PLAIN)
        s = s * score_scale + jnp.concatenate(masks, axis=1)
        scores[j] = s
        return jnp.maximum(highest, jnp.maximum(s[:, :block], s[:, block:]))

    highest = lax.fori_loop(0, pairs, score, jnp.full((rows, block), -jnp.inf, jnp.float32))
    ns = dot(query, fresh[:, :latent], LAST) + dot(query_r, fresh[:, latent:], LAST)
    column = lax.broadcasted_iota(jnp.int32, ns.shape, 1)
    step_of = lax.broadcasted_iota(jnp.int32, ns.shape, 0) // total[1]
    ns = jnp.where(column <= step_of, ns * score_scale, -jnp.inf)
    top = jnp.maximum(
        jnp.max(highest, axis=1, keepdims=True), jnp.max(ns, axis=1, keepdims=True)
    )
    nw = jnp.exp(ns - top)
    acc = total[0]
    acc[...] = dot(nw.astype(jnp.bfloat16), fresh[:, :latent], PLAIN)

    def mix(j, sums):
        w = jnp.exp(scores[j] - top)
        keys = latv[pl.ds(2 * j, 2)][:, :block, :].reshape(2 * block, latent)
        acc[...] += dot(w.astype(jnp.bfloat16), keys, PLAIN)
        return sums + (w[:, :block] + w[:, block:])

    sums = lax.fori_loop(0, pairs, mix, jnp.zeros((rows, block), jnp.float32))
    weight_sum = jnp.sum(sums, axis=1, keepdims=True) + jnp.sum(nw, axis=1, keepdims=True)
    return (acc[...] / weight_sum).astype(jnp.bfloat16)


def turned(rope):
    return rope.astype(jnp.float32).T.astype(jnp.bfloat16)


def owned_kernel(by_fill, slot, has_base, table, count, length, q_lat, q_rope, new, *refs):
    refs = list(refs)
    lat = refs.pop(0)
    rope = None if by_fill else refs.pop(0)
    if has_base:
        refs.pop(0)
    out, latv = refs.pop(0), refs.pop(0)
    ropev = None if by_fill else refs.pop(0)
    scores, acc, done, sem, out_sem = refs

    def copies(i, b):
        made = [pltpu.make_async_copy(lat.at[b], latv.at[i], sem.at[0, i])]
        if not by_fill:
            made.append(pltpu.make_async_copy(rope.at[b], ropev.at[i], sem.at[1, i]))
        return made

    steps, heads, latent = q_lat.shape[1:]
    query = q_lat[0].reshape(steps * heads, latent)
    query_r = jnp.concatenate([turned(q_rope[0, t]) for t in range(steps)], axis=0)
    fresh = new[0].astype(jnp.float32)
    fresh = jnp.concatenate(
        [fresh, jnp.zeros((FRESH - steps, fresh.shape[1]), jnp.float32)], axis=0
    ).astype(jnp.bfloat16)
    value = attention(
        by_fill, table, count[0], length[0], latv, ropev, sem, copies, query, query_r, fresh, scores,
        (acc, heads),
    )
    done[...] = value.reshape(steps, heads, latent)
    back = pltpu.make_async_copy(done, out.at[slot], out_sem.at[0])
    back.start()
    back.wait()


def owned(slot, table, count, length, q_lat, q_rope, new_kv, lat, rope, base=None):
    by_fill = rope is None
    steps, heads, latent = q_lat.shape[1:]
    rows = steps * heads
    width, block = q_rope.shape[2], heads if by_fill else lat.shape[1]
    if by_fill:
        block = lat.shape[1] * latent // (latent + width)
    listed = table.shape[0] + table.shape[0] % 2
    smem = pl.BlockSpec(memory_space=pltpu.SMEM)
    far = pl.BlockSpec(memory_space=pl.ANY)
    operands = [table, count, length, q_lat, q_rope, new_kv, lat]
    specs = [smem] * 3 + [pick(slot, a) for a in (q_lat, q_rope, new_kv)] + [far]
    scratch = [pltpu.VMEM((listed,) + lat.shape[1:], jnp.bfloat16)]
    if not by_fill:
        operands.append(rope)
        specs.append(far)
        scratch.append(pltpu.VMEM((listed,) + rope.shape[1:], jnp.bfloat16))
    aliases = {}
    if base is not None:
        aliases = {len(operands): 0}
        operands.append(base)
        specs.append(far)
    return pl.pallas_call(
        functools.partial(owned_kernel, by_fill, slot, base is not None),
        grid=(1,),
        out_shape=jax.ShapeDtypeStruct(q_lat.shape, jnp.bfloat16),
        in_specs=specs,
        out_specs=far,
        scratch_shapes=scratch
        + [
            pltpu.VMEM((listed // 2, rows, 2 * block), jnp.float32),
            pltpu.VMEM((rows, latent), jnp.float32),
            pltpu.VMEM((steps, heads, latent), jnp.bfloat16),
            pltpu.SemaphoreType.DMA((2, listed)),
            pltpu.SemaphoreType.DMA((2,)),
        ],
        input_output_aliases=aliases,
        compiler_params=pltpu.CompilerParams(vmem_limit_bytes=24 * 2**20 if by_fill else VMEM_BYTES),
        cost_estimate=pl.CostEstimate(
            flops=2 * rows * listed * block * (2 * latent + width),
            bytes_accessed=lat.size * 2 + rows * latent * 4,
            transcendentals=rows * listed * block,
        ),
    )(*operands)


def swap(bit, value, beside=None):
    size = lax.axis_size("dp")

    def branch(level, operand):
        route = [(low, low ^ (1 << max(level, 0))) for low in range(size)]
        got = operand if level < 0 else lax.ppermute(operand, "dp", route)
        return got if beside is None else (got, beside())

    levels = range(-1, size.bit_length() - 1)
    return lax.switch(bit + 1, [functools.partial(branch, level) for level in levels], value)


def fetch(bit, mine, theirs, kept, block):
    size = lax.axis_size("dp")
    most = kept.shape[0]
    quarter = -(-most // 4)
    levels = size.bit_length() - 1
    level_of = jnp.maximum(bit, 0)
    low_here = jnp.bitwise_and(jnp.right_shift(lax.axis_index("dp"), level_of), 1) == 0

    def quarters(length):
        return jnp.clip((length + block - 1) // block - 1, 0, most - 1) // quarter

    up = quarters(jnp.where(low_here, mine, theirs))
    down = quarters(jnp.where(low_here, theirs, mine))

    def branch(level, up_quarters, down_quarters, operand):
        lows = [i for i in range(size) if not i >> level & 1]
        up_count = min(up_quarters * quarter, most)
        down_count = min(down_quarters * quarter, most)
        rising = lax.ppermute(operand[:up_count], "dp", [(i, i | 1 << level) for i in lows])
        falling = lax.ppermute(operand[:down_count], "dp", [(i | 1 << level, i) for i in lows])
        rest = ((0, 0), (0, 0))
        return jnp.where(
            low_here,
            jnp.pad(falling, ((0, most - down_count),) + rest),
            jnp.pad(rising, ((0, most - up_count),) + rest),
        )

    branches = [lambda operand: operand] + [
        functools.partial(branch, level, up_quarters, down_quarters)
        for level in range(levels)
        for up_quarters in range(1, 5)
        for down_quarters in range(1, 5)
    ]
    return lax.switch(jnp.where(bit < 0, 0, 1 + (level_of * 4 + up) * 4 + down), branches, kept)


def shards(
    res_lat,
    res_rope,
    res_table,
    res_len,
    out_lat,
    out_rope,
    out_fill,
    send_table,
    arr_index,
    arr_count,
    mig_lat,
    mig_rope,
    mig_len,
    mig_bit,
    q_lat,
    q_rope,
    new_kv,
):
    block_len = res_lat.shape[1]
    requests = res_len.shape[0]
    moved = requests + 1

    def blocks_of(length):
        return (length + block_len - 1) // block_len

    theirs, (sent, kept) = swap(
        mig_bit[0],
        mig_len,
        lambda: pack_blocks(send_table, out_fill, mig_len, out_lat, out_rope, mig_lat, mig_rope),
    )
    cache = fetch(mig_bit[0], mig_len[0], theirs[0], kept, block_len)
    sent, cache = lax.optimization_barrier((sent, cache))
    got = lax.all_to_all(sent, "dp", split_axis=0, concat_axis=0, tiled=True)

    out = None
    for r in range(requests):
        length = res_len[r : r + 1]
        out = owned(
            r, res_table[r], blocks_of(length), length, q_lat, q_rope, new_kv, res_lat, res_rope, base=out
        )
    straight = jnp.arange(mig_lat.shape[0], dtype=jnp.int32)
    out = owned(
        moved, straight, blocks_of(theirs), theirs, q_lat, q_rope, new_kv, cache, None, base=out
    )
    return owned(
        requests, arr_index, arr_count, arr_count, q_lat, q_rope, new_kv, got, None, base=out
    )


def solution(mesh):
    both = ("groups", "dp")
    ranks = (3, 3, 2, 1, 3, 3, 1, 1, 1, 1, 3, 3, 1, 1, 4, 4, 3)
    return jax.shard_map(
        shards,
        mesh=mesh,
        in_specs=tuple(P(both, *([None] * (rank - 1))) for rank in ranks),
        out_specs=P(both, None, None, None),
        check_vma=False,
    )
```

```python
import functools

import jax
import jax.numpy as jnp
from jax import lax
from jax.experimental import pallas as pl
from jax.experimental.pallas import tpu as pltpu
from jax.sharding import PartitionSpec as P

score_scale = 192.0 ** (-0.5)
EXTRA = 8
FRESH = 16
LAST = (((1,), (1,)), ((), ()))
PLAIN = (((1,), (0,)), ((), ()))
VMEM_BYTES = 56 * 2**20


def dot(a, b, dims):
    return lax.dot_general(a, b, dims, preferred_element_type=jnp.float32)


def fold(rope, latent):
    parts = latent // rope.shape[1]
    each = rope.shape[0] // parts
    return jnp.concatenate([rope[p * each : (p + 1) * each] for p in range(parts)], axis=1)


def unfold(folded, width):
    parts = folded.shape[1] // width
    return jnp.concatenate([folded[:, p * width : (p + 1) * width] for p in range(parts)], axis=0)


def blocks_kernel(table, fills, lat, rope, sent):
    slots, latent = sent.shape[0], sent.shape[2]
    block = lat.shape[1]
    lane = lax.broadcasted_iota(jnp.int32, rope.shape[1:], 1)

    def slot(s, carry):
        b = table[s]

        @pl.when(b >= 0)
        def _():
            sent[s, :block, :] = lat[b]
            marked = jnp.where(lane < fills[b], rope[b].astype(jnp.float32), jnp.inf)
            sent[s, block:, :] = fold(marked.astype(jnp.bfloat16), latent)

        return carry

    lax.fori_loop(0, slots, slot, 0)


def payload_kernel(q_lat, q_rope, new, payload):
    steps, heads = q_lat.shape[1:3]
    latent = payload.shape[2]
    folded = payload.shape[1] - heads - EXTRA
    fresh = new[0].astype(jnp.float32)
    width = fresh.shape[1] - latent
    for t in range(steps):
        payload[t, :heads, :] = q_lat[0, t]
        payload[t, heads : heads + folded, :] = fold(q_rope[0, t], latent)
        rope_row = jnp.concatenate(
            [fresh[t : t + 1, latent:], jnp.zeros((1, latent - width), jnp.float32)], axis=1
        )
        payload[t, heads + folded :, :] = jnp.concatenate(
            [fresh[t : t + 1, :latent], rope_row, jnp.zeros((EXTRA - 2, latent), jnp.float32)], axis=0
        ).astype(jnp.bfloat16)


def pick(slot, array):
    rest = array.shape[1:]
    return pl.BlockSpec((1,) + rest, lambda i: (slot,) + (0,) * len(rest))


def whole(array):
    return pl.BlockSpec(array.shape, lambda i: (0,) * len(array.shape))


def pack_blocks(send_table, out_fill, out_lat, out_rope):
    block, latent = out_lat.shape[1:]
    folded = out_rope.shape[1] * out_rope.shape[2] // latent
    smem = pl.BlockSpec(memory_space=pltpu.SMEM)
    shape = jax.ShapeDtypeStruct((send_table.shape[0], block + folded, latent), jnp.bfloat16)
    return pl.pallas_call(
        blocks_kernel,
        grid=(1,),
        out_shape=shape,
        in_specs=[smem, smem, whole(out_lat), whole(out_rope)],
        out_specs=whole(shape),
        compiler_params=pltpu.CompilerParams(vmem_limit_bytes=VMEM_BYTES),
        cost_estimate=pl.CostEstimate(flops=0, bytes_accessed=shape.size * 4, transcendentals=0),
    )(send_table, out_fill, out_lat, out_rope)


def pack_payload(q_lat, q_rope, new_kv, moved):
    steps, heads, latent = q_lat.shape[1:]
    folded = q_rope.shape[2] * heads // latent
    shape = jax.ShapeDtypeStruct((steps, heads + folded + EXTRA, latent), jnp.bfloat16)
    return pl.pallas_call(
        payload_kernel,
        grid=(1,),
        out_shape=shape,
        in_specs=[pick(moved, a) for a in (q_lat, q_rope, new_kv)],
        out_specs=whole(shape),
        compiler_params=pltpu.CompilerParams(vmem_limit_bytes=VMEM_BYTES),
    )(q_lat, q_rope, new_kv)


def attention(
    by_fill, table, count, length, latv, ropev, sem, copies, query, query_r, fresh, scores, total
):
    rows, latent = query.shape
    width = query_r.shape[1]
    block = scores.shape[2] // 2
    lane = lax.broadcasted_iota(jnp.int32, (1, block), 1)

    def begin(i, carry):
        for copy in copies(i, table[i]):
            copy.start()
        return carry

    lax.fori_loop(0, count, begin, 0)
    pairs = (count + 1) // 2

    @pl.when(count % 2 == 1)
    def _():
        latv[count] = jnp.zeros(latv.shape[1:], latv.dtype)
        if ropev is not None:
            ropev[count] = jnp.zeros(ropev.shape[1:], ropev.dtype)

    def score(j, highest):
        ropes, masks = [], []
        for half in range(2):
            i = 2 * j + half

            @pl.when(i < count)
            def _():
                for copy in copies(i, table[i]):
                    copy.wait()

        for half in range(2):
            i = 2 * j + half
            if by_fill:
                carried = unfold(latv[i, block:, :], block).astype(jnp.float32)
                marked = carried < jnp.inf
                ropes.append(jnp.where(marked, carried, 0.0).astype(jnp.bfloat16))
                masks.append(jnp.where(marked[:1] & (i < count), 0.0, -jnp.inf))
            else:
                ropes.append(ropev[i])
                masks.append(jnp.where(lane + i * block < length, 0.0, -jnp.inf))
        keys = latv[pl.ds(2 * j, 2)][:, :block, :].reshape(2 * block, latent)
        s = dot(query, keys, LAST) + dot(query_r, jnp.concatenate(ropes, axis=1), PLAIN)
        s = s * score_scale + jnp.concatenate(masks, axis=1)
        scores[j] = s
        return jnp.maximum(highest, jnp.maximum(s[:, :block], s[:, block:]))

    highest = lax.fori_loop(0, pairs, score, jnp.full((rows, block), -jnp.inf, jnp.float32))
    ns = dot(query, fresh[:, :latent], LAST) + dot(query_r, fresh[:, latent:], LAST)
    column = lax.broadcasted_iota(jnp.int32, ns.shape, 1)
    step_of = lax.broadcasted_iota(jnp.int32, ns.shape, 0) // total[1]
    ns = jnp.where(column <= step_of, ns * score_scale, -jnp.inf)
    top = jnp.maximum(
        jnp.max(highest, axis=1, keepdims=True), jnp.max(ns, axis=1, keepdims=True)
    )
    nw = jnp.exp(ns - top)
    acc = total[0]
    acc[...] = dot(nw.astype(jnp.bfloat16), fresh[:, :latent], PLAIN)

    def mix(j, sums):
        w = jnp.exp(scores[j] - top)
        keys = latv[pl.ds(2 * j, 2)][:, :block, :].reshape(2 * block, latent)
        acc[...] += dot(w.astype(jnp.bfloat16), keys, PLAIN)
        return sums + (w[:, :block] + w[:, block:])

    sums = lax.fori_loop(0, pairs, mix, jnp.zeros((rows, block), jnp.float32))
    weight_sum = jnp.sum(sums, axis=1, keepdims=True) + jnp.sum(nw, axis=1, keepdims=True)
    return (acc[...] / weight_sum).astype(jnp.bfloat16)


def turned(rope):
    return rope.astype(jnp.float32).T.astype(jnp.bfloat16)


def owned_kernel(by_fill, table, count, length, q_lat, q_rope, new, *refs):
    refs = list(refs)
    lat = refs.pop(0)
    rope = None if by_fill else refs.pop(0)
    out, latv = refs.pop(0), refs.pop(0)
    ropev = None if by_fill else refs.pop(0)
    scores, acc, sem = refs

    def copies(i, b):
        made = [pltpu.make_async_copy(lat.at[b], latv.at[i], sem.at[0, i])]
        if not by_fill:
            made.append(pltpu.make_async_copy(rope.at[b], ropev.at[i], sem.at[1, i]))
        return made

    steps, heads, latent = q_lat.shape[1:]
    query = q_lat[0].reshape(steps * heads, latent)
    query_r = jnp.concatenate([turned(q_rope[0, t]) for t in range(steps)], axis=0)
    fresh = new[0].astype(jnp.float32)
    fresh = jnp.concatenate(
        [fresh, jnp.zeros((FRESH - steps, fresh.shape[1]), jnp.float32)], axis=0
    ).astype(jnp.bfloat16)
    value = attention(
        by_fill, table, count[0], length[0], latv, ropev, sem, copies, query, query_r, fresh, scores,
        (acc, heads),
    )
    out[...] = value.reshape(steps, heads, latent)


def owned(slot, table, count, length, q_lat, q_rope, new_kv, lat, rope):
    by_fill = rope is None
    steps, heads, latent = q_lat.shape[1:]
    rows = steps * heads
    width, block = q_rope.shape[2], heads if by_fill else lat.shape[1]
    if by_fill:
        block = lat.shape[1] * latent // (latent + width)
    listed = table.shape[0] + table.shape[0] % 2
    smem = pl.BlockSpec(memory_space=pltpu.SMEM)
    far = pl.BlockSpec(memory_space=pl.ANY)
    operands = [table, count, length, q_lat, q_rope, new_kv, lat]
    specs = [smem] * 3 + [pick(slot, a) for a in (q_lat, q_rope, new_kv)] + [far]
    scratch = [pltpu.VMEM((listed,) + lat.shape[1:], jnp.bfloat16)]
    if not by_fill:
        operands.append(rope)
        specs.append(far)
        scratch.append(pltpu.VMEM((listed,) + rope.shape[1:], jnp.bfloat16))
    shape = jax.ShapeDtypeStruct(q_lat.shape[1:], jnp.bfloat16)
    return pl.pallas_call(
        functools.partial(owned_kernel, by_fill),
        grid=(1,),
        out_shape=shape,
        in_specs=specs,
        out_specs=whole(shape),
        scratch_shapes=scratch
        + [
            pltpu.VMEM((listed // 2, rows, 2 * block), jnp.float32),
            pltpu.VMEM((rows, latent), jnp.float32),
            pltpu.SemaphoreType.DMA((2, listed)),
        ],
        compiler_params=pltpu.CompilerParams(vmem_limit_bytes=24 * 2**20 if by_fill else VMEM_BYTES),
        cost_estimate=pl.CostEstimate(
            flops=2 * rows * listed * block * (2 * latent + width),
            bytes_accessed=lat.size * 2 + rows * latent * 4,
            transcendentals=rows * listed * block,
        ),
    )(*operands)


def visitor_kernel(width, length, payload, lat, rope, out, latv, ropev, scores, acc, sem):
    steps, heads, latent = out.shape
    block = lat.shape[1]
    folded = width * heads // latent
    top = heads + folded

    def copies(i, b):
        return [
            pltpu.make_async_copy(lat.at[b], latv.at[i], sem.at[0, i]),
            pltpu.make_async_copy(rope.at[b], ropev.at[i], sem.at[1, i]),
        ]

    query = payload[:, :heads, :].reshape(steps * heads, latent)
    query_r = jnp.concatenate(
        [turned(unfold(payload[t, heads:top, :], heads)) for t in range(steps)], axis=0
    )
    tails = [payload[t, top:, :].astype(jnp.float32) for t in range(steps)]
    fresh = jnp.concatenate(
        [jnp.concatenate([tail[0:1], tail[1:2, :width]], axis=1) for tail in tails]
        + [jnp.zeros((FRESH - steps, latent + width), jnp.float32)],
        axis=0,
    ).astype(jnp.bfloat16)
    count = (length[0] + block - 1) // block
    value = attention(
        False, lambda_table, count, length[0], latv, ropev, sem, copies, query, query_r, fresh, scores,
        (acc, heads),
    )
    out[...] = value.reshape(steps, heads, latent)


class Straight:
    def __getitem__(self, i):
        return i


lambda_table = Straight()


def visited(length, payload, lat, rope, heads):
    steps, latent = payload.shape[0], payload.shape[2]
    rows = steps * heads
    blocks, width, block = rope.shape
    listed = blocks + blocks % 2
    far = pl.BlockSpec(memory_space=pl.ANY)
    shape = jax.ShapeDtypeStruct((steps, heads, latent), jnp.bfloat16)
    return pl.pallas_call(
        functools.partial(visitor_kernel, width),
        grid=(1,),
        out_shape=shape,
        in_specs=[pl.BlockSpec(memory_space=pltpu.SMEM), whole(payload), far, far],
        out_specs=whole(shape),
        scratch_shapes=[
            pltpu.VMEM((listed,) + lat.shape[1:], jnp.bfloat16),
            pltpu.VMEM((listed,) + rope.shape[1:], jnp.bfloat16),
            pltpu.VMEM((listed // 2, rows, 2 * block), jnp.float32),
            pltpu.VMEM((rows, latent), jnp.float32),
            pltpu.SemaphoreType.DMA((2, listed)),
        ],
        compiler_params=pltpu.CompilerParams(vmem_limit_bytes=VMEM_BYTES),
        cost_estimate=pl.CostEstimate(
            flops=2 * rows * listed * block * (2 * latent + width),
            bytes_accessed=lat.size * 2 + rows * latent * 4,
            transcendentals=rows * listed * block,
        ),
    )(length, payload, lat, rope)


def swap(bit, value, beside=None):
    size = lax.axis_size("dp")

    def branch(level, operand):
        route = [(low, low ^ (1 << max(level, 0))) for low in range(size)]
        got = operand if level < 0 else lax.ppermute(operand, "dp", route)
        return got if beside is None else (got, beside())

    levels = range(-1, size.bit_length() - 1)
    return lax.switch(bit + 1, [functools.partial(branch, level) for level in levels], value)


def shards(
    res_lat,
    res_rope,
    res_table,
    res_len,
    out_lat,
    out_rope,
    out_fill,
    send_table,
    arr_index,
    arr_count,
    mig_lat,
    mig_rope,
    mig_len,
    mig_bit,
    q_lat,
    q_rope,
    new_kv,
):
    block_len = res_lat.shape[1]
    requests = res_len.shape[0]
    heads = q_lat.shape[2]
    moved = requests + 1

    sent = pack_blocks(send_table, out_fill, out_lat, out_rope)
    got = lax.all_to_all(sent, "dp", split_axis=0, concat_axis=0, tiled=True)
    payload = pack_payload(q_lat, q_rope, new_kv, moved)

    def residents():
        outs = []
        for r in range(requests):
            length = res_len[r : r + 1]
            outs.append(
                owned(
                    r, res_table[r], (length + block_len - 1) // block_len, length, q_lat, q_rope,
                    new_kv, res_lat, res_rope,
                )
            )
        return outs

    def arrival():
        return owned(
            requests, arr_index, arr_count, arr_count, q_lat, q_rope, new_kv, got, None
        )

    visitor, outs = swap(mig_bit[0], payload, residents)
    computed = visited(mig_len, visitor, mig_lat, mig_rope, heads)
    moved_out, arrival_out = swap(mig_bit[0], computed, arrival)
    return jnp.stack(outs + [arrival_out, moved_out])


def solution(mesh):
    both = ("groups", "dp")
    ranks = (3, 3, 2, 1, 3, 3, 1, 1, 1, 1, 3, 3, 1, 1, 4, 4, 3)
    return jax.shard_map(
        shards,
        mesh=mesh,
        in_specs=tuple(P(both, *([None] * (rank - 1))) for rank in ranks),
        out_specs=P(both, None, None, None),
        check_vma=False,
    )
```

```python
import functools

import jax
import jax.numpy as jnp
from jax import lax
from jax.experimental import pallas as pl
from jax.experimental.pallas import tpu as pltpu
from jax.sharding import PartitionSpec as P

score_scale = 192.0 ** (-0.5)
EXTRA = 8
FRESH = 16
LAST = (((1,), (1,)), ((), ()))
PLAIN = (((1,), (0,)), ((), ()))
VMEM_BYTES = 56 * 2**20


def dot(a, b, dims):
    return lax.dot_general(a, b, dims, preferred_element_type=jnp.float32)


def fold(rope, latent):
    parts = latent // rope.shape[1]
    each = rope.shape[0] // parts
    return jnp.concatenate([rope[p * each : (p + 1) * each] for p in range(parts)], axis=1)


def unfold(folded, width):
    parts = folded.shape[1] // width
    return jnp.concatenate([folded[:, p * width : (p + 1) * width] for p in range(parts)], axis=0)


def blocks_kernel(table, fills, lat, rope, sent):
    slots, latent = sent.shape[0], sent.shape[2]
    block = lat.shape[1]
    lane = lax.broadcasted_iota(jnp.int32, rope.shape[1:], 1)

    def slot(s, carry):
        b = table[s]

        @pl.when(b >= 0)
        def _():
            sent[s, :block, :] = lat[b]
            marked = jnp.where(lane < fills[b], rope[b].astype(jnp.float32), jnp.inf)
            sent[s, block:, :] = fold(marked.astype(jnp.bfloat16), latent)

        return carry

    lax.fori_loop(0, slots, slot, 0)


def payload_kernel(q_lat, q_rope, new, payload):
    steps, heads = q_lat.shape[1:3]
    latent = payload.shape[2]
    folded = payload.shape[1] - heads - EXTRA
    fresh = new[0].astype(jnp.float32)
    width = fresh.shape[1] - latent
    for t in range(steps):
        payload[t, :heads, :] = q_lat[0, t]
        payload[t, heads : heads + folded, :] = fold(q_rope[0, t], latent)
        rope_row = jnp.concatenate(
            [fresh[t : t + 1, latent:], jnp.zeros((1, latent - width), jnp.float32)], axis=1
        )
        payload[t, heads + folded :, :] = jnp.concatenate(
            [fresh[t : t + 1, :latent], rope_row, jnp.zeros((EXTRA - 2, latent), jnp.float32)], axis=0
        ).astype(jnp.bfloat16)


def pick(slot, array):
    rest = array.shape[1:]
    return pl.BlockSpec((1,) + rest, lambda i: (slot,) + (0,) * len(rest))


def whole(array):
    return pl.BlockSpec(array.shape, lambda i: (0,) * len(array.shape))


def pack_blocks(send_table, out_fill, out_lat, out_rope):
    block, latent = out_lat.shape[1:]
    folded = out_rope.shape[1] * out_rope.shape[2] // latent
    smem = pl.BlockSpec(memory_space=pltpu.SMEM)
    shape = jax.ShapeDtypeStruct((send_table.shape[0], block + folded, latent), jnp.bfloat16)
    return pl.pallas_call(
        blocks_kernel,
        grid=(1,),
        out_shape=shape,
        in_specs=[smem, smem, whole(out_lat), whole(out_rope)],
        out_specs=whole(shape),
        compiler_params=pltpu.CompilerParams(vmem_limit_bytes=VMEM_BYTES),
        cost_estimate=pl.CostEstimate(flops=0, bytes_accessed=shape.size * 4, transcendentals=0),
    )(send_table, out_fill, out_lat, out_rope)


def pack_payload(q_lat, q_rope, new_kv, moved):
    steps, heads, latent = q_lat.shape[1:]
    folded = q_rope.shape[2] * heads // latent
    shape = jax.ShapeDtypeStruct((steps, heads + folded + EXTRA, latent), jnp.bfloat16)
    return pl.pallas_call(
        payload_kernel,
        grid=(1,),
        out_shape=shape,
        in_specs=[pick(moved, a) for a in (q_lat, q_rope, new_kv)],
        out_specs=whole(shape),
        compiler_params=pltpu.CompilerParams(vmem_limit_bytes=VMEM_BYTES),
    )(q_lat, q_rope, new_kv)


def attention(
    by_fill, table, count, length, latv, ropev, sem, copies, query, query_r, fresh, scores, total
):
    rows, latent = query.shape
    width = query_r.shape[1]
    block = scores.shape[2] // 2
    lane = lax.broadcasted_iota(jnp.int32, (1, block), 1)

    def begin(i, carry):
        for copy in copies(i, table[i]):
            copy.start()
        return carry

    lax.fori_loop(0, count, begin, 0)
    pairs = (count + 1) // 2

    @pl.when(count % 2 == 1)
    def _():
        latv[count] = jnp.zeros(latv.shape[1:], latv.dtype)
        if ropev is not None:
            ropev[count] = jnp.zeros(ropev.shape[1:], ropev.dtype)

    def score(j, highest):
        ropes, masks = [], []
        for half in range(2):
            i = 2 * j + half

            @pl.when(i < count)
            def _():
                for copy in copies(i, table[i]):
                    copy.wait()

        for half in range(2):
            i = 2 * j + half
            if by_fill:
                carried = unfold(latv[i, block:, :], block).astype(jnp.float32)
                marked = carried < jnp.inf
                ropes.append(jnp.where(marked, carried, 0.0).astype(jnp.bfloat16))
                masks.append(jnp.where(marked[:1] & (i < count), 0.0, -jnp.inf))
            else:
                ropes.append(ropev[i])
                masks.append(jnp.where(lane + i * block < length, 0.0, -jnp.inf))
        keys = latv[pl.ds(2 * j, 2)][:, :block, :].reshape(2 * block, latent)
        s = dot(query, keys, LAST) + dot(query_r, jnp.concatenate(ropes, axis=1), PLAIN)
        s = s * score_scale + jnp.concatenate(masks, axis=1)
        scores[j] = s
        return jnp.maximum(highest, jnp.maximum(s[:, :block], s[:, block:]))

    highest = lax.fori_loop(0, pairs, score, jnp.full((rows, block), -jnp.inf, jnp.float32))
    ns = dot(query, fresh[:, :latent], LAST) + dot(query_r, fresh[:, latent:], LAST)
    column = lax.broadcasted_iota(jnp.int32, ns.shape, 1)
    step_of = lax.broadcasted_iota(jnp.int32, ns.shape, 0) // total[1]
    ns = jnp.where(column <= step_of, ns * score_scale, -jnp.inf)
    top = jnp.maximum(
        jnp.max(highest, axis=1, keepdims=True), jnp.max(ns, axis=1, keepdims=True)
    )
    nw = jnp.exp(ns - top)
    acc = total[0]
    acc[...] = dot(nw.astype(jnp.bfloat16), fresh[:, :latent], PLAIN)

    def mix(j, sums):
        w = jnp.exp(scores[j] - top)
        keys = latv[pl.ds(2 * j, 2)][:, :block, :].reshape(2 * block, latent)
        acc[...] += dot(w.astype(jnp.bfloat16), keys, PLAIN)
        return sums + (w[:, :block] + w[:, block:])

    sums = lax.fori_loop(0, pairs, mix, jnp.zeros((rows, block), jnp.float32))
    weight_sum = jnp.sum(sums, axis=1, keepdims=True) + jnp.sum(nw, axis=1, keepdims=True)
    return (acc[...] / weight_sum).astype(jnp.bfloat16)


def turned(rope):
    return rope.astype(jnp.float32).T.astype(jnp.bfloat16)


def owned_kernel(by_fill, table, count, length, q_lat, q_rope, new, *refs):
    refs = list(refs)
    lat = refs.pop(0)
    rope = None if by_fill else refs.pop(0)
    out, latv = refs.pop(0), refs.pop(0)
    ropev = None if by_fill else refs.pop(0)
    scores, acc, sem = refs

    def copies(i, b):
        made = [pltpu.make_async_copy(lat.at[b], latv.at[i], sem.at[0, i])]
        if not by_fill:
            made.append(pltpu.make_async_copy(rope.at[b], ropev.at[i], sem.at[1, i]))
        return made

    steps, heads, latent = q_lat.shape[1:]
    query = q_lat[0].reshape(steps * heads, latent)
    query_r = jnp.concatenate([turned(q_rope[0, t]) for t in range(steps)], axis=0)
    fresh = new[0].astype(jnp.float32)
    fresh = jnp.concatenate(
        [fresh, jnp.zeros((FRESH - steps, fresh.shape[1]), jnp.float32)], axis=0
    ).astype(jnp.bfloat16)
    value = attention(
        by_fill, table, count[0], length[0], latv, ropev, sem, copies, query, query_r, fresh, scores,
        (acc, heads),
    )
    out[...] = value.reshape(steps, heads, latent)


def owned(slot, table, count, length, q_lat, q_rope, new_kv, lat, rope):
    by_fill = rope is None
    steps, heads, latent = q_lat.shape[1:]
    rows = steps * heads
    width, block = q_rope.shape[2], heads if by_fill else lat.shape[1]
    if by_fill:
        block = lat.shape[1] * latent // (latent + width)
    listed = table.shape[0] + table.shape[0] % 2
    smem = pl.BlockSpec(memory_space=pltpu.SMEM)
    far = pl.BlockSpec(memory_space=pl.ANY)
    operands = [table, count, length, q_lat, q_rope, new_kv, lat]
    specs = [smem] * 3 + [pick(slot, a) for a in (q_lat, q_rope, new_kv)] + [far]
    scratch = [pltpu.VMEM((listed,) + lat.shape[1:], jnp.bfloat16)]
    if not by_fill:
        operands.append(rope)
        specs.append(far)
        scratch.append(pltpu.VMEM((listed,) + rope.shape[1:], jnp.bfloat16))
    shape = jax.ShapeDtypeStruct(q_lat.shape[1:], jnp.bfloat16)
    return pl.pallas_call(
        functools.partial(owned_kernel, by_fill),
        grid=(1,),
        out_shape=shape,
        in_specs=specs,
        out_specs=whole(shape),
        scratch_shapes=scratch
        + [
            pltpu.VMEM((listed // 2, rows, 2 * block), jnp.float32),
            pltpu.VMEM((rows, latent), jnp.float32),
            pltpu.SemaphoreType.DMA((2, listed)),
        ],
        compiler_params=pltpu.CompilerParams(vmem_limit_bytes=24 * 2**20 if by_fill else VMEM_BYTES),
        cost_estimate=pl.CostEstimate(
            flops=2 * rows * listed * block * (2 * latent + width),
            bytes_accessed=lat.size * 2 + rows * latent * 4,
            transcendentals=rows * listed * block,
        ),
    )(*operands)


def visitor_kernel(width, length, payload, lat, rope, out, latv, ropev, scores, acc, sem):
    steps, heads, latent = out.shape
    block = lat.shape[1]
    folded = width * heads // latent
    top = heads + folded

    def copies(i, b):
        return [
            pltpu.make_async_copy(lat.at[b], latv.at[i], sem.at[0, i]),
            pltpu.make_async_copy(rope.at[b], ropev.at[i], sem.at[1, i]),
        ]

    query = payload[:, :heads, :].reshape(steps * heads, latent)
    query_r = jnp.concatenate(
        [turned(unfold(payload[t, heads:top, :], heads)) for t in range(steps)], axis=0
    )
    tails = [payload[t, top:, :].astype(jnp.float32) for t in range(steps)]
    fresh = jnp.concatenate(
        [jnp.concatenate([tail[0:1], tail[1:2, :width]], axis=1) for tail in tails]
        + [jnp.zeros((FRESH - steps, latent + width), jnp.float32)],
        axis=0,
    ).astype(jnp.bfloat16)
    count = (length[0] + block - 1) // block
    value = attention(
        False, lambda_table, count, length[0], latv, ropev, sem, copies, query, query_r, fresh, scores,
        (acc, heads),
    )
    out[...] = value.reshape(steps, heads, latent)


class Straight:
    def __getitem__(self, i):
        return i


lambda_table = Straight()


def visited(length, payload, lat, rope, heads):
    steps, latent = payload.shape[0], payload.shape[2]
    rows = steps * heads
    blocks, width, block = rope.shape
    listed = blocks + blocks % 2
    far = pl.BlockSpec(memory_space=pl.ANY)
    shape = jax.ShapeDtypeStruct((steps, heads, latent), jnp.bfloat16)
    return pl.pallas_call(
        functools.partial(visitor_kernel, width),
        grid=(1,),
        out_shape=shape,
        in_specs=[pl.BlockSpec(memory_space=pltpu.SMEM), whole(payload), far, far],
        out_specs=whole(shape),
        scratch_shapes=[
            pltpu.VMEM((listed,) + lat.shape[1:], jnp.bfloat16),
            pltpu.VMEM((listed,) + rope.shape[1:], jnp.bfloat16),
            pltpu.VMEM((listed // 2, rows, 2 * block), jnp.float32),
            pltpu.VMEM((rows, latent), jnp.float32),
            pltpu.SemaphoreType.DMA((2, listed)),
        ],
        compiler_params=pltpu.CompilerParams(vmem_limit_bytes=VMEM_BYTES),
        cost_estimate=pl.CostEstimate(
            flops=2 * rows * listed * block * (2 * latent + width),
            bytes_accessed=lat.size * 2 + rows * latent * 4,
            transcendentals=rows * listed * block,
        ),
    )(length, payload, lat, rope)


def swap(bit, value, beside=None):
    size = lax.axis_size("dp")

    def branch(level, operand):
        route = [(low, low ^ (1 << max(level, 0))) for low in range(size)]
        got = operand if level < 0 else lax.ppermute(operand, "dp", route)
        return got if beside is None else (got, beside())

    levels = range(-1, size.bit_length() - 1)
    return lax.switch(bit + 1, [functools.partial(branch, level) for level in levels], value)


def shards(
    res_lat,
    res_rope,
    res_table,
    res_len,
    out_lat,
    out_rope,
    out_fill,
    send_table,
    arr_index,
    arr_count,
    mig_lat,
    mig_rope,
    mig_len,
    mig_bit,
    q_lat,
    q_rope,
    new_kv,
):
    block_len = res_lat.shape[1]
    requests = res_len.shape[0]
    heads = q_lat.shape[2]
    moved = requests + 1

    payload = pack_payload(q_lat, q_rope, new_kv, moved)
    visitor, sent = swap(
        mig_bit[0], payload, lambda: pack_blocks(send_table, out_fill, out_lat, out_rope)
    )
    sent, visitor = lax.optimization_barrier((sent, visitor))
    got = lax.all_to_all(sent, "dp", split_axis=0, concat_axis=0, tiled=True)

    def residents():
        outs = []
        for r in range(requests):
            length = res_len[r : r + 1]
            outs.append(
                owned(
                    r, res_table[r], (length + block_len - 1) // block_len, length, q_lat, q_rope,
                    new_kv, res_lat, res_rope,
                )
            )
        return outs

    def arrival():
        return owned(
            requests, arr_index, arr_count, arr_count, q_lat, q_rope, new_kv, got, None
        )

    computed = visited(mig_len, visitor, mig_lat, mig_rope, heads)
    computed, outs = lax.optimization_barrier((computed, residents()))
    moved_out, arrival_out = swap(mig_bit[0], computed, arrival)
    return jnp.stack(outs + [arrival_out, moved_out])


def solution(mesh):
    both = ("groups", "dp")
    ranks = (3, 3, 2, 1, 3, 3, 1, 1, 1, 1, 3, 3, 1, 1, 4, 4, 3)
    return jax.shard_map(
        shards,
        mesh=mesh,
        in_specs=tuple(P(both, *([None] * (rank - 1))) for rank in ranks),
        out_specs=P(both, None, None, None),
        check_vma=False,
    )
```

```python
import functools

import jax
import jax.numpy as jnp
from jax import lax
from jax.experimental import pallas as pl
from jax.experimental.pallas import tpu as pltpu
from jax.sharding import PartitionSpec as P

score_scale = 192.0 ** (-0.5)
EXTRA = 8
FRESH = 16
LAST = (((1,), (1,)), ((), ()))
PLAIN = (((1,), (0,)), ((), ()))
VMEM_BYTES = 56 * 2**20


def dot(a, b, dims):
    return lax.dot_general(a, b, dims, preferred_element_type=jnp.float32)


def fold(rope, latent):
    parts = latent // rope.shape[1]
    each = rope.shape[0] // parts
    return jnp.concatenate([rope[p * each : (p + 1) * each] for p in range(parts)], axis=1)


def unfold(folded, width):
    parts = folded.shape[1] // width
    return jnp.concatenate([folded[:, p * width : (p + 1) * width] for p in range(parts)], axis=0)


def blocks_kernel(table, fills, lat, rope, sent):
    slots, latent = sent.shape[0], sent.shape[2]
    block = lat.shape[1]
    lane = lax.broadcasted_iota(jnp.int32, rope.shape[1:], 1)

    def slot(s, carry):
        b = table[s]

        @pl.when(b >= 0)
        def _():
            sent[s, :block, :] = lat[b]
            marked = jnp.where(lane < fills[b], rope[b].astype(jnp.float32), jnp.inf)
            sent[s, block:, :] = fold(marked.astype(jnp.bfloat16), latent)

        return carry

    lax.fori_loop(0, slots, slot, 0)


def payload_kernel(q_lat, q_rope, new, payload):
    steps, heads = q_lat.shape[1:3]
    latent = payload.shape[2]
    folded = payload.shape[1] - heads - EXTRA
    fresh = new[0].astype(jnp.float32)
    width = fresh.shape[1] - latent
    for t in range(steps):
        payload[t, :heads, :] = q_lat[0, t]
        payload[t, heads : heads + folded, :] = fold(q_rope[0, t], latent)
        rope_row = jnp.concatenate(
            [fresh[t : t + 1, latent:], jnp.zeros((1, latent - width), jnp.float32)], axis=1
        )
        payload[t, heads + folded :, :] = jnp.concatenate(
            [fresh[t : t + 1, :latent], rope_row, jnp.zeros((EXTRA - 2, latent), jnp.float32)], axis=0
        ).astype(jnp.bfloat16)


def pick(slot, array):
    rest = array.shape[1:]
    return pl.BlockSpec((1,) + rest, lambda i: (slot,) + (0,) * len(rest))


def whole(array):
    return pl.BlockSpec(array.shape, lambda i: (0,) * len(array.shape))


def pack_blocks(send_table, out_fill, out_lat, out_rope):
    block, latent = out_lat.shape[1:]
    folded = out_rope.shape[1] * out_rope.shape[2] // latent
    smem = pl.BlockSpec(memory_space=pltpu.SMEM)
    shape = jax.ShapeDtypeStruct((send_table.shape[0], block + folded, latent), jnp.bfloat16)
    return pl.pallas_call(
        blocks_kernel,
        grid=(1,),
        out_shape=shape,
        in_specs=[smem, smem, whole(out_lat), whole(out_rope)],
        out_specs=whole(shape),
        compiler_params=pltpu.CompilerParams(vmem_limit_bytes=VMEM_BYTES),
        cost_estimate=pl.CostEstimate(flops=0, bytes_accessed=shape.size * 4, transcendentals=0),
    )(send_table, out_fill, out_lat, out_rope)


def pack_payload(q_lat, q_rope, new_kv, moved):
    steps, heads, latent = q_lat.shape[1:]
    folded = q_rope.shape[2] * heads // latent
    shape = jax.ShapeDtypeStruct((steps, heads + folded + EXTRA, latent), jnp.bfloat16)
    return pl.pallas_call(
        payload_kernel,
        grid=(1,),
        out_shape=shape,
        in_specs=[pick(moved, a) for a in (q_lat, q_rope, new_kv)],
        out_specs=whole(shape),
        compiler_params=pltpu.CompilerParams(vmem_limit_bytes=VMEM_BYTES),
    )(q_lat, q_rope, new_kv)


def attention(
    by_fill, table, count, length, latv, ropev, sem, copies, query, query_r, fresh, scores, total
):
    rows, latent = query.shape
    width = query_r.shape[1]
    block = scores.shape[2] // 2
    lane = lax.broadcasted_iota(jnp.int32, (1, block), 1)

    def begin(i, carry):
        for copy in copies(i, table[i]):
            copy.start()
        return carry

    lax.fori_loop(0, count, begin, 0)
    pairs = (count + 1) // 2

    @pl.when(count % 2 == 1)
    def _():
        latv[count] = jnp.zeros(latv.shape[1:], latv.dtype)
        if ropev is not None:
            ropev[count] = jnp.zeros(ropev.shape[1:], ropev.dtype)

    def score(j, highest):
        ropes, masks = [], []
        for half in range(2):
            i = 2 * j + half

            @pl.when(i < count)
            def _():
                for copy in copies(i, table[i]):
                    copy.wait()

        for half in range(2):
            i = 2 * j + half
            if by_fill:
                carried = unfold(latv[i, block:, :], block).astype(jnp.float32)
                marked = carried < jnp.inf
                ropes.append(jnp.where(marked, carried, 0.0).astype(jnp.bfloat16))
                masks.append(jnp.where(marked[:1] & (i < count), 0.0, -jnp.inf))
            else:
                ropes.append(ropev[i])
                masks.append(jnp.where(lane + i * block < length, 0.0, -jnp.inf))
        keys = latv[pl.ds(2 * j, 2)][:, :block, :].reshape(2 * block, latent)
        s = dot(query, keys, LAST) + dot(query_r, jnp.concatenate(ropes, axis=1), PLAIN)
        s = s * score_scale + jnp.concatenate(masks, axis=1)
        scores[j] = s
        return jnp.maximum(highest, jnp.maximum(s[:, :block], s[:, block:]))

    highest = lax.fori_loop(0, pairs, score, jnp.full((rows, block), -jnp.inf, jnp.float32))
    ns = dot(query, fresh[:, :latent], LAST) + dot(query_r, fresh[:, latent:], LAST)
    column = lax.broadcasted_iota(jnp.int32, ns.shape, 1)
    step_of = lax.broadcasted_iota(jnp.int32, ns.shape, 0) // total[1]
    ns = jnp.where(column <= step_of, ns * score_scale, -jnp.inf)
    top = jnp.maximum(
        jnp.max(highest, axis=1, keepdims=True), jnp.max(ns, axis=1, keepdims=True)
    )
    nw = jnp.exp(ns - top)
    acc = total[0]
    acc[...] = dot(nw.astype(jnp.bfloat16), fresh[:, :latent], PLAIN)

    def mix(j, sums):
        w = jnp.exp(scores[j] - top)
        keys = latv[pl.ds(2 * j, 2)][:, :block, :].reshape(2 * block, latent)
        acc[...] += dot(w.astype(jnp.bfloat16), keys, PLAIN)
        return sums + (w[:, :block] + w[:, block:])

    sums = lax.fori_loop(0, pairs, mix, jnp.zeros((rows, block), jnp.float32))
    weight_sum = jnp.sum(sums, axis=1, keepdims=True) + jnp.sum(nw, axis=1, keepdims=True)
    return (acc[...] / weight_sum).astype(jnp.bfloat16)


def turned(rope):
    return rope.astype(jnp.float32).T.astype(jnp.bfloat16)


def owned_kernel(by_fill, table, count, length, q_lat, q_rope, new, *refs):
    refs = list(refs)
    lat = refs.pop(0)
    rope = None if by_fill else refs.pop(0)
    out, latv = refs.pop(0), refs.pop(0)
    ropev = None if by_fill else refs.pop(0)
    scores, acc, sem = refs

    def copies(i, b):
        made = [pltpu.make_async_copy(lat.at[b], latv.at[i], sem.at[0, i])]
        if not by_fill:
            made.append(pltpu.make_async_copy(rope.at[b], ropev.at[i], sem.at[1, i]))
        return made

    steps, heads, latent = q_lat.shape[1:]
    query = q_lat[0].reshape(steps * heads, latent)
    query_r = jnp.concatenate([turned(q_rope[0, t]) for t in range(steps)], axis=0)
    fresh = new[0].astype(jnp.float32)
    fresh = jnp.concatenate(
        [fresh, jnp.zeros((FRESH - steps, fresh.shape[1]), jnp.float32)], axis=0
    ).astype(jnp.bfloat16)
    value = attention(
        by_fill, table, count[0], length[0], latv, ropev, sem, copies, query, query_r, fresh, scores,
        (acc, heads),
    )
    out[...] = value.reshape(steps, heads, latent)


def owned(slot, table, count, length, q_lat, q_rope, new_kv, lat, rope):
    by_fill = rope is None
    steps, heads, latent = q_lat.shape[1:]
    rows = steps * heads
    width, block = q_rope.shape[2], heads if by_fill else lat.shape[1]
    if by_fill:
        block = lat.shape[1] * latent // (latent + width)
    listed = table.shape[0] + table.shape[0] % 2
    smem = pl.BlockSpec(memory_space=pltpu.SMEM)
    far = pl.BlockSpec(memory_space=pl.ANY)
    operands = [table, count, length, q_lat, q_rope, new_kv, lat]
    specs = [smem] * 3 + [pick(slot, a) for a in (q_lat, q_rope, new_kv)] + [far]
    scratch = [pltpu.VMEM((listed,) + lat.shape[1:], jnp.bfloat16)]
    if not by_fill:
        operands.append(rope)
        specs.append(far)
        scratch.append(pltpu.VMEM((listed,) + rope.shape[1:], jnp.bfloat16))
    shape = jax.ShapeDtypeStruct(q_lat.shape[1:], jnp.bfloat16)
    return pl.pallas_call(
        functools.partial(owned_kernel, by_fill),
        grid=(1,),
        out_shape=shape,
        in_specs=specs,
        out_specs=whole(shape),
        scratch_shapes=scratch
        + [
            pltpu.VMEM((listed // 2, rows, 2 * block), jnp.float32),
            pltpu.VMEM((rows, latent), jnp.float32),
            pltpu.SemaphoreType.DMA((2, listed)),
        ],
        compiler_params=pltpu.CompilerParams(vmem_limit_bytes=24 * 2**20 if by_fill else VMEM_BYTES),
        cost_estimate=pl.CostEstimate(
            flops=2 * rows * listed * block * (2 * latent + width),
            bytes_accessed=lat.size * 2 + rows * latent * 4,
            transcendentals=rows * listed * block,
        ),
    )(*operands)


def visitor_kernel(width, length, payload, lat, rope, out, latv, ropev, scores, acc, sem):
    steps, heads, latent = out.shape
    block = lat.shape[1]
    folded = width * heads // latent
    top = heads + folded

    def copies(i, b):
        return [
            pltpu.make_async_copy(lat.at[b], latv.at[i], sem.at[0, i]),
            pltpu.make_async_copy(rope.at[b], ropev.at[i], sem.at[1, i]),
        ]

    query = payload[:, :heads, :].reshape(steps * heads, latent)
    query_r = jnp.concatenate(
        [turned(unfold(payload[t, heads:top, :], heads)) for t in range(steps)], axis=0
    )
    tails = [payload[t, top:, :].astype(jnp.float32) for t in range(steps)]
    fresh = jnp.concatenate(
        [jnp.concatenate([tail[0:1], tail[1:2, :width]], axis=1) for tail in tails]
        + [jnp.zeros((FRESH - steps, latent + width), jnp.float32)],
        axis=0,
    ).astype(jnp.bfloat16)
    count = (length[0] + block - 1) // block
    value = attention(
        False, lambda_table, count, length[0], latv, ropev, sem, copies, query, query_r, fresh, scores,
        (acc, heads),
    )
    out[...] = value.reshape(steps, heads, latent)


class Straight:
    def __getitem__(self, i):
        return i


lambda_table = Straight()


def visited(length, payload, lat, rope, heads):
    steps, latent = payload.shape[0], payload.shape[2]
    rows = steps * heads
    blocks, width, block = rope.shape
    listed = blocks + blocks % 2
    far = pl.BlockSpec(memory_space=pl.ANY)
    shape = jax.ShapeDtypeStruct((steps, heads, latent), jnp.bfloat16)
    return pl.pallas_call(
        functools.partial(visitor_kernel, width),
        grid=(1,),
        out_shape=shape,
        in_specs=[pl.BlockSpec(memory_space=pltpu.SMEM), whole(payload), far, far],
        out_specs=whole(shape),
        scratch_shapes=[
            pltpu.VMEM((listed,) + lat.shape[1:], jnp.bfloat16),
            pltpu.VMEM((listed,) + rope.shape[1:], jnp.bfloat16),
            pltpu.VMEM((listed // 2, rows, 2 * block), jnp.float32),
            pltpu.VMEM((rows, latent), jnp.float32),
            pltpu.SemaphoreType.DMA((2, listed)),
        ],
        compiler_params=pltpu.CompilerParams(vmem_limit_bytes=VMEM_BYTES),
        cost_estimate=pl.CostEstimate(
            flops=2 * rows * listed * block * (2 * latent + width),
            bytes_accessed=lat.size * 2 + rows * latent * 4,
            transcendentals=rows * listed * block,
        ),
    )(length, payload, lat, rope)


def swap(bit, value, beside=None):
    size = lax.axis_size("dp")

    def branch(level, operand):
        route = [(low, low ^ (1 << max(level, 0))) for low in range(size)]
        got = operand if level < 0 else lax.ppermute(operand, "dp", route)
        return got if beside is None else (got, beside())

    levels = range(-1, size.bit_length() - 1)
    return lax.switch(bit + 1, [functools.partial(branch, level) for level in levels], value)


def shards(
    res_lat,
    res_rope,
    res_table,
    res_len,
    out_lat,
    out_rope,
    out_fill,
    send_table,
    arr_index,
    arr_count,
    mig_lat,
    mig_rope,
    mig_len,
    mig_bit,
    q_lat,
    q_rope,
    new_kv,
):
    block_len = res_lat.shape[1]
    requests = res_len.shape[0]
    heads = q_lat.shape[2]
    moved = requests + 1

    payload = pack_payload(q_lat, q_rope, new_kv, moved)
    visitor, sent = swap(
        mig_bit[0], payload, lambda: pack_blocks(send_table, out_fill, out_lat, out_rope)
    )
    sent, visitor = lax.optimization_barrier((sent, visitor))
    got = lax.all_to_all(sent, "dp", split_axis=0, concat_axis=0, tiled=True)

    def residents():
        outs = []
        for r in range(requests):
            length = res_len[r : r + 1]
            outs.append(
                owned(
                    r, res_table[r], (length + block_len - 1) // block_len, length, q_lat, q_rope,
                    new_kv, res_lat, res_rope,
                )
            )
        return outs

    def arrival(got):
        return owned(
            requests, arr_index, arr_count, arr_count, q_lat, q_rope, new_kv, got, None
        )

    computed = visited(mig_len, visitor, mig_lat, mig_rope, heads)
    moved_out, outs = swap(mig_bit[0], computed, residents)
    got, moved_out = lax.optimization_barrier((got, moved_out))
    return jnp.stack(outs + [arrival(got), moved_out])


def solution(mesh):
    both = ("groups", "dp")
    ranks = (3, 3, 2, 1, 3, 3, 1, 1, 1, 1, 3, 3, 1, 1, 4, 4, 3)
    return jax.shard_map(
        shards,
        mesh=mesh,
        in_specs=tuple(P(both, *([None] * (rank - 1))) for rank in ranks),
        out_specs=P(both, None, None, None),
        check_vma=False,
    )
```
